32 devices in a mesh: section: 4 (over z), dp: 8 (over y, x, core).
Axes of the slice: x: 2, y: 2, z: 4, core: 2. Of those that a mesh axis runs over, the one named last changes fastest.
Arguments:
- inputs: bfloat16 [2, 1024, 2048], P(None, 'dp', 'section'), may hold values from -6 to 6
- cotangent: bfloat16 [2, 1024, 2048], P(None, 'dp', 'section'), may hold values from -6 to 6
- resets: int32 [2, 1024], replicated, may hold values from 0 to 1, as said below
- branch_in: bfloat16 [2, 2048, 2560], P(None, 'dp'), may hold values from -0.125 to 0.125
- gate_in: bfloat16 [2, 2048, 2560], P(None, 'dp'), may hold values from -0.125 to 0.125
- rec_out: bfloat16 [2, 2560, 2048], P(None, 'dp'), may hold values from -0.5 to 0.5
- rate_gate: bfloat16 [2, 10, 256, 256], P(None, None, 'dp'), may hold values from -0.375 to 0.375
- input_gate: bfloat16 [2, 10, 256, 256], P(None, None, 'dp'), may hold values from -0.375 to 0.375
- conv_taps: bfloat16 [2, 4, 2560], P(None, None, 'dp'), may hold values from -3 to 3
- conv_bias: bfloat16 [2, 2560], P(None, 'dp'), may hold values from -3 to 3
- rate_bias: bfloat16 [2, 2560], P(None, 'dp'), may hold values from -4 to 4
- input_bias: bfloat16 [2, 2560], P(None, 'dp'), may hold values from -4 to 4
- decay_param: bfloat16 [2, 2560], P(None, 'dp'), may hold values from 4 to 12
- norm_rec: bfloat16 [2, 2048], P(None, 'dp'), may hold values from 0.5 to 1.5
- norm_mlp: bfloat16 [2, 2048], P(None, 'dp'), may hold values from 0.5 to 1.5
- mlp_gate: bfloat16 [2, 2048, 6144], P(None, 'dp'), may hold values from -0.125 to 0.125
- mlp_up: bfloat16 [2, 2048, 6144], P(None, 'dp'), may hold values from -0.125 to 0.125
- mlp_down: bfloat16 [2, 6144, 2048], P(None, 'dp'), may hold values from -0.15625 to 0.15625
Outputs:
- output: bfloat16 [2, 1024, 2048], P(None, 'dp', 'section')
- input_grad: bfloat16 [2, 1024, 2048], P(None, 'dp', 'section')
- grad_branch_in: float32 [2, 2048, 2560], P(None, 'dp')
- grad_gate_in: float32 [2, 2048, 2560], P(None, 'dp')
- grad_rec_out: float32 [2, 2560, 2048], P(None, 'dp')
- grad_rate_gate: float32 [2, 10, 256, 256], P(None, None, 'dp')
- grad_input_gate: float32 [2, 10, 256, 256], P(None, None, 'dp')
- grad_conv_taps: float32 [2, 4, 2560], P(None, None, 'dp')
- grad_conv_bias: float32 [2, 2560], P(None, 'dp')
- grad_rate_bias: float32 [2, 2560], P(None, 'dp')
- grad_input_bias: float32 [2, 2560], P(None, 'dp')
- grad_decay_param: float32 [2, 2560], P(None, 'dp')
- grad_norm_rec: float32 [2, 2048], P(None, 'dp')
- grad_norm_mlp: float32 [2, 2048], P(None, 'dp')
- grad_mlp_gate: float32 [2, 2048, 6144], P(None, 'dp')
- grad_mlp_up: float32 [2, 2048, 6144], P(None, 'dp')
- grad_mlp_down: float32 [2, 6144, 2048], P(None, 'dp')
The draws below stay inside these ranges and needn't reach their ends.
Inputs may be any that keep to these rules, and one draw needn't show every extreme that they name: `resets`: every micro-batch has a 1 at position 0. In one micro-batch, chosen by the seed, a row starts within the first half of 128 positions and the next row starts within the last half of 128 positions, with no other row start between; the other starts fall at random positions.
All inputs are finite; a program needn't handle non-finite values.
Results may differ from the reference program's by a relative error of at most 0.018.
Values may be sent and summed in bfloat16 or wider, within the bound.
No kernel may reach another device: no remote copies, remote signals or barrier semaphores. Data moves between devices by JAX's collectives and lax.ppermute only.
A program may use at most 640 MiB of HBM per device.

```python
import jax
import jax.numpy as jnp
from jax import lax

D = 2048
H = 10
BW = 256
F = 6144
R = 2560
CONV = 4
MICRO = 2
SHORT = 512
TOK_MB = 128
LAYERS = 2
SEQ = 1024


def draw_resets(key, part):
    key = jax.random.fold_in(key, 7)
    subkeys = jax.random.split(key, 4)
    starts = (jax.random.randint(subkeys[0], (MICRO, SEQ), 0, SHORT) == 0).astype(jnp.int32)
    reach_max = max(TOK_MB // 2, 1)
    long_start = jax.random.randint(subkeys[1], (), 1, reach_max + 1)
    finish = SEQ - jax.random.randint(subkeys[2], (), 1, reach_max + 1)
    chosen = jax.random.randint(subkeys[3], (), 0, MICRO)
    position = jnp.arange(SEQ)
    inside = (position > long_start) & (position < finish)
    boundary = (position == long_start) | (position == finish)
    long_rows = jnp.where(inside[None, :], 0, jnp.where(boundary[None, :], 1, starts))
    chosen_row = (jnp.arange(MICRO) == chosen)[:, None]
    flagged = jnp.where(chosen_row, long_rows, starts)
    return jnp.where(position[None, :] == 0, 1, flagged).astype(jnp.int32)


def steps_of(rng, shape, cuts, smallest, largest):
    def one(dim, parts):
        steps = jax.random.uniform(jax.random.fold_in(jax.random.fold_in(rng, 6), dim), (parts,), jnp.float32, smallest / len(cuts), largest / len(cuts))
        return jnp.repeat(jnp.exp(steps), shape[dim] // parts).reshape((-1,) + (1,) * (len(shape) - dim - 1))

    level = one(*cuts[0])
    for cut in cuts[1:]:
        level = level * one(*cut)
    return level


def scatter_about(rng, extent, width, limit, pieces=(), held_as=jnp.bfloat16):
    factor_of = steps_of(rng, extent, pieces, -0.22, 0.18) if pieces else 1.0
    values = jax.random.normal(rng, extent, jnp.float32) * width * factor_of
    return jnp.minimum(jnp.maximum(values, -limit), limit).astype(held_as)


def setup_inputs(seed: int = 0) -> dict:
    arg_keys = jax.random.split(jax.random.key(seed), 19)
    return {
        "inputs": scatter_about(arg_keys[0], (MICRO, SEQ, D), 1.0, 6.0, ((1, 8), (2, 4))),
        "cotangent": scatter_about(arg_keys[1], (MICRO, SEQ, D), 1.0, 6.0, ((1, 8), (2, 4))),
        "resets": draw_resets(jax.random.fold_in(arg_keys[18], 71), 0),
        "branch_in": scatter_about(arg_keys[3], (LAYERS, D, R), D ** -0.5, 0.125, ((1, 8),)),
        "gate_in": scatter_about(arg_keys[4], (LAYERS, D, R), D ** -0.5, 0.125, ((1, 8),)),
        "rec_out": scatter_about(arg_keys[5], (LAYERS, R, D), (R // 16) ** -0.5, 0.5, ((1, 8),)),
        "rate_gate": scatter_about(arg_keys[6], (LAYERS, H, BW, BW), BW ** -0.5, 0.375, ((2, 8),)),
        "input_gate": scatter_about(arg_keys[7], (LAYERS, H, BW, BW), BW ** -0.5, 0.375, ((2, 8),)),
        "conv_taps": scatter_about(arg_keys[8], (LAYERS, CONV, R), CONV ** -0.5, 3.0, ((2, 8),)),
        "conv_bias": scatter_about(arg_keys[9], (LAYERS, R), 0.5, 3.0, ((1, 8),)),
        "rate_bias": scatter_about(arg_keys[10], (LAYERS, R), 1.0, 4.0, ((1, 8),)),
        "input_bias": scatter_about(arg_keys[11], (LAYERS, R), 1.0, 4.0, ((1, 8),)),
        "decay_param": jnp.clip(4.0 + 8.0 * jax.random.uniform(arg_keys[12], (LAYERS, R), jnp.float32) ** steps_of(arg_keys[12], (LAYERS, R), ((1, 8),), -0.2, 0.2), 4.0, 12.0).astype(jnp.bfloat16),
        "norm_rec": jnp.clip(1.0 + 0.1 * jax.random.normal(arg_keys[13], (LAYERS, D), jnp.float32), 0.5, 1.5).astype(jnp.bfloat16),
        "norm_mlp": jnp.clip(1.0 + 0.1 * jax.random.normal(arg_keys[14], (LAYERS, D), jnp.float32), 0.5, 1.5).astype(jnp.bfloat16),
        "mlp_gate": scatter_about(arg_keys[15], (LAYERS, D, F), D ** -0.5, 0.125, ((1, 8),)),
        "mlp_up": scatter_about(arg_keys[16], (LAYERS, D, F), D ** -0.5, 0.125, ((1, 8),)),
        "mlp_down": scatter_about(arg_keys[17], (LAYERS, F, D), (F // 4) ** -0.5, 0.15625, ((1, 8),)),
    }


EPS = 1e-06
LRU_EPS = 0.04
RATE_SCALE = 8.0
HIGHEST = lax.Precision.HIGHEST

@jax.custom_vjp
def low(v):
    return lax.optimization_barrier(v.astype(jnp.bfloat16)).astype(jnp.float32)

@jax.custom_vjp
def low_back(v):
    return v

def low_keep(v):
    return (low(v), None)

def low_pass(kept, grad):
    return (grad,)

def back_keep(v):
    return (v, None)

def back_low(kept, grad):
    return (low(grad),)
low.defvjp(low_keep, low_pass)
low_back.defvjp(back_keep, back_low)

def rms_scale(values, scales):
    return values * lax.rsqrt(lax.optimization_barrier(jnp.mean(values * values, axis=-1, keepdims=True)) + EPS) * scales

def product(left, right):
    return jnp.matmul(left, right, precision=HIGHEST)

def block_product(values, blocks):
    leading = values.shape[:-1]
    split = values.reshape(leading + (H, BW))
    return jnp.einsum('msha,hab->mshb', split, blocks, precision=HIGHEST).reshape(leading + (R,))

def shifted(values, offset, padding):
    filler = jnp.full(values.shape[:1] + (offset,) + values.shape[2:], padding, values.dtype)
    return jnp.concatenate([filler, values[:, :values.shape[1] - offset]], axis=1)

def lru_step(carried, pair):
    decays, drives = pair
    updated = decays * carried + drives
    return (updated, updated)

def rec_block(stream, carry_mask, params):
    branch_in, gate_in, rec_out, rate_gate, input_gate, conv_taps, conv_bias, rate_bias, input_bias, decay_param, norm_rec, norm_mlp, mlp_gate, mlp_up, mlp_down = params
    normed = low(rms_scale(stream, norm_rec))
    branch = low_back(product(normed, branch_in))
    side = low_back(product(normed, gate_in))
    conved = conv_bias + conv_taps[0] * branch
    usable = jnp.ones_like(carry_mask)
    for lag_steps in range(1, CONV):
        usable = usable * shifted(carry_mask, lag_steps - 1, 1.0)
        conved = conved + conv_taps[lag_steps] * usable * shifted(branch, lag_steps, 0.0)
    conv_low = low(conved)
    rate_pre = low_back(block_product(conv_low, rate_gate)) + rate_bias
    input_pre = low_back(block_product(conv_low, input_gate)) + input_bias
    decays = jnp.exp(-RATE_SCALE * jax.nn.softplus(-decay_param) * jax.nn.sigmoid(rate_pre)) * carry_mask
    drives = jnp.sqrt(1.0 + LRU_EPS - decays * decays) * jax.nn.sigmoid(input_pre) * conved
    initial = jnp.zeros((stream.shape[0], R), jnp.float32)
    _, states = lax.scan(lru_step, initial, (jnp.swapaxes(decays, 0, 1), jnp.swapaxes(drives, 0, 1)))
    states = jnp.swapaxes(states, 0, 1)
    mixture = low(states * jax.nn.gelu(side))
    return stream + low_back(product(mixture, rec_out))

def mlp_block(stream, params):
    branch_in, gate_in, rec_out, rate_gate, input_gate, conv_taps, conv_bias, rate_bias, input_bias, decay_param, norm_rec, norm_mlp, mlp_gate, mlp_up, mlp_down = params
    normed_mlp = low(rms_scale(stream, norm_mlp))
    gate_val = low_back(product(normed_mlp, mlp_gate))
    up_val = low_back(product(normed_mlp, mlp_up))
    hidden = low(jax.nn.gelu(gate_val) * up_val)
    return stream + low_back(product(hidden, mlp_down))

def reference(inputs, cotangent, resets, branch_in, gate_in, rec_out, rate_gate, input_gate, conv_taps, conv_bias, rate_bias, input_bias, decay_param, norm_rec, norm_mlp, mlp_gate, mlp_up, mlp_down):
    carry_mask = (1 - resets).astype(jnp.float32)[:, :, None]
    params = tuple((weight.astype(jnp.float32) for weight in (branch_in, gate_in, rec_out, rate_gate, input_gate, conv_taps, conv_bias, rate_bias, input_bias, decay_param, norm_rec, norm_mlp, mlp_gate, mlp_up, mlp_down)))

    def forward(stream, weights):
        for layer_index in range(LAYERS):
            layer_params = tuple((weight[layer_index] for weight in weights))
            stream = jax.checkpoint(rec_block)(stream, carry_mask, layer_params)
            stream = low_back(low(stream))
            stream = jax.checkpoint(mlp_block)(stream, layer_params)
            if layer_index + 1 < LAYERS:
                stream = low_back(low(stream))
        return stream
    result, pullback = jax.vjp(forward, inputs.astype(jnp.float32), params)
    grad_stream, grads = pullback(cotangent.astype(jnp.float32))
    return (result.astype(jnp.bfloat16), grad_stream.astype(jnp.bfloat16), grads[0], grads[1], grads[2], grads[3], grads[4], grads[5], grads[6], grads[7], grads[8], grads[9], grads[10], grads[11], grads[12], grads[13], grads[14])
```

```python
import jax
import jax.numpy as jnp
from jax import lax
from jax.experimental import pallas as pl
from jax.experimental.pallas import tpu as pltpu
from jax.sharding import PartitionSpec as P

D = 2048
H = 10
BW = 256
F = 6144
R = 2560
CONV = 4
MICRO = 2
LAYERS = 2
MARGIN = CONV - 1
WIN = 2 * BW

EPS = 1e-06
LRU_EPS = 0.04
RATE_SCALE = 8.0


def low(value):
    return value.astype(jnp.bfloat16)


def high(value):
    return value.astype(jnp.float32)


def dot(left, right):
    return jnp.dot(left, right, preferred_element_type=jnp.float32)


def dot_nt(left, right):
    return lax.dot_general(
        left, right, (((1,), (1,)), ((), ())), preferred_element_type=jnp.float32
    )


def dot_tn(left, right):
    return lax.dot_general(
        left, right, (((0,), (0,)), ((), ())), preferred_element_type=jnp.float32
    )


def rms_scale(values, scales):
    return values * lax.rsqrt(jnp.mean(values * values, axis=-1, keepdims=True) + EPS) * scales


def meeting_order(count):
    return list(range(0, count, 2)) + list(range(1, count, 2))


def swapped(value, offset):
    count = lax.axis_size("dp")
    return lax.ppermute(value, "dp", [(at, at ^ offset) for at in range(count)])


def gather_rows(block):
    count = lax.axis_size("dp")
    same_core = jnp.concatenate([block] + [swapped(block, k) for k in range(2, count, 2)], axis=0)
    other_core = swapped(same_core, 1)
    return jnp.concatenate([same_core, other_core], axis=0)


def scatter_product(product, left):
    count = lax.axis_size("dp")
    half = left.shape[0] // 2
    rows = left.shape[0] // count
    away = swapped(low(product(left[half:])), 1)
    here = product(left[:half]) + high(away)
    total = here[:rows]
    for k in range(2, count, 2):
        piece = here[(k // 2) * rows : (k // 2 + 1) * rows]
        total = total + high(swapped(low(piece), k))
    return total


def spread(pack):
    return lax.all_to_all(pack, "dp", 0, 0, tiled=False)


def section_sum(chunks):
    rank = lax.axis_index("section")
    pick = lambda value, at: lax.dynamic_index_in_dim(value, at, 0, keepdims=False)
    part = lambda value, at, size: lax.dynamic_slice_in_dim(value, at, size, 0)
    first = lax.ppermute(
        part(chunks, jnp.where(rank == 0, 1, 0), 3), "section", [(0, 1), (3, 2)]
    )
    second_own = part(chunks, jnp.where(rank == 1, 2, 0), 2)
    second_came = part(first, jnp.where(rank == 1, 1, 0), 2)
    second = lax.ppermute(
        low(high(second_own) + high(second_came)), "section", [(1, 2), (2, 1)]
    )
    lower_half = rank == 1
    third = lax.ppermute(
        low(
            high(pick(chunks, jnp.where(lower_half, 0, 3)))
            + high(pick(second, jnp.where(lower_half, 0, 1)))
        ),
        "section",
        [(1, 0), (2, 3)],
    )
    return (
        high(pick(chunks, rank))
        + high(pick(first, jnp.where(lower_half, 0, 2)))
        + high(pick(second, jnp.where(lower_half, 1, 0)))
        + high(third)
    )


def window_of(device, count):
    own = R // count
    first_block = min(own * device // BW, H - 2)
    return own * device, own * (device + 1), BW * first_block, BW * first_block + WIN


def own_first(matrix, device, count):
    begin, end, left, right = window_of(device, count)
    return [matrix[:, begin:end], matrix[:, end:right], matrix[:, left:begin]]


def turned(value, axis, shift):
    size = value.shape[axis]
    twice = jnp.concatenate([value, value], axis=axis)
    return lax.dynamic_slice_in_dim(twice, jnp.mod(shift, size), size, axis)


def forward_scan_kernel(decay_ref, drive_ref, reach_ref, state_ref):
    rows = decay_ref.shape[1]
    reach = decay_ref[:, 0, :]
    state = drive_ref[:, 0, :]
    reach_ref[:, 0, :] = reach
    state_ref[:, 0, :] = state
    for row in range(1, rows):
        decay = decay_ref[:, row, :]
        state = decay * state + drive_ref[:, row, :]
        reach = decay * reach
        reach_ref[:, row, :] = reach
        state_ref[:, row, :] = state


def backward_scan_kernel(decay_ref, grad_ref, reach_ref, local_ref, top_ref):
    rows = decay_ref.shape[1]
    reach = jnp.ones_like(decay_ref[:, 0, :])
    local = grad_ref[:, rows - 1, :]
    reach_ref[:, rows - 1, :] = reach
    local_ref[:, rows - 1, :] = local
    for row in range(rows - 2, -1, -1):
        decay = decay_ref[:, row + 1, :]
        local = decay * local + grad_ref[:, row, :]
        reach = decay * reach
        reach_ref[:, row, :] = reach
        local_ref[:, row, :] = local
    top_ref[0] = decay_ref[:, 0, :] * reach
    top_ref[1] = decay_ref[:, 0, :] * local


def carry_kernel(reverse, where_ref, totals_ref, carry_ref):
    planes, count = totals_ref.shape[0], totals_ref.shape[2]
    me, rank = where_ref[0], where_ref[1]
    state = jnp.zeros(carry_ref.shape[1:], jnp.float32)
    for step in range(count):
        device = count - 1 - step if reverse else step
        offset = jnp.bitwise_xor(me, device)
        at = offset // 2 + (offset % 2) * (count // 2)
        for plane in range(planes - 1, -1, -1) if reverse else range(planes):

            @pl.when(rank == plane)
            def _(state=state, at=at):
                carry_ref[at] = state

            state = totals_ref[plane, 0, at] * state + totals_ref[plane, 1, at]


VMEM_SPEC = pl.BlockSpec(memory_space=pltpu.VMEM)


def in_vmem(kernel, shapes, *operands, scalars=0):
    specs = [pl.BlockSpec(memory_space=pltpu.SMEM)] * scalars
    return pl.pallas_call(
        kernel,
        out_shape=tuple(jax.ShapeDtypeStruct(shape, jnp.float32) for shape in shapes),
        in_specs=specs + [VMEM_SPEC] * (len(operands) - scalars),
        out_specs=tuple(VMEM_SPEC for _ in shapes),
        compiler_params=pltpu.CompilerParams(vmem_limit_bytes=40 * 1024 * 1024),
    )(*operands)


def carried(totals, reverse):
    count = lax.axis_size("dp")
    channels = totals.shape[-1]
    everything = lax.all_gather(
        totals.reshape(2, count, MICRO, channels), "section", axis=0, tiled=False
    )
    where = jnp.stack([lax.axis_index("dp"), lax.axis_index("section")]).astype(jnp.int32)

    def kernel(where_ref, totals_ref, carry_ref):
        carry_kernel(reverse, where_ref, totals_ref, carry_ref)

    (carry,) = in_vmem(kernel, [(count, MICRO, channels)], where, everything, scalars=1)
    return carry.reshape(count * MICRO, channels)


def gelu_product(states, side):
    return states * jax.nn.gelu(side)


def gated_gelu(gate_val, up_val):
    return jax.nn.gelu(gate_val) * up_val


def local(
    inputs,
    cotangent,
    resets,
    branch_in,
    gate_in,
    rec_out,
    rate_gate,
    input_gate,
    conv_taps,
    conv_bias,
    rate_bias,
    input_bias,
    decay_param,
    norm_rec,
    norm_mlp,
    mlp_gate,
    mlp_up,
    mlp_down,
):
    planes = lax.axis_size("section")
    count = lax.axis_size("dp")
    rank = lax.axis_index("section")
    me = lax.axis_index("dp")
    block_rows = inputs.shape[1]
    length = block_rows // planes
    seq = resets.shape[1]
    rows = MICRO * length
    segments = MICRO * count
    tokens = segments * length
    own = R // count
    wide = F // count
    strip = D // count
    thin = strip // planes
    order = jnp.array(meeting_order(count), jnp.int32)
    devices = jnp.bitwise_xor(me, order)

    small = jnp.concatenate(
        [
            norm_rec,
            norm_mlp,
            conv_taps.reshape(LAYERS, CONV * own),
            conv_bias,
        ],
        axis=1,
    )
    small_all = lax.all_gather(small, "dp", axis=0, tiled=False)
    own_begin = own * me
    first_block = jnp.minimum(own_begin // BW, H - 2)
    shift = own_begin - BW * first_block

    def small_whole(layer, begin, each):
        return small_all[:, layer, begin : begin + each].reshape(count * each)

    weights = []
    for layer in range(LAYERS):
        in_pack = jnp.stack(
            [
                jnp.concatenate(
                    own_first(branch_in[layer], device, count)
                    + [gate_in[layer][:, own * device : own * (device + 1)]],
                    axis=1,
                )
                for device in range(count)
            ]
        )
        gates = jnp.stack([rate_gate[layer], input_gate[layer]])
        gate_pack = jnp.stack(
            [
                gates[:, window_of(device, count)[2] // BW : window_of(device, count)[3] // BW]
                for device in range(count)
            ]
        )
        mlp_pack = jnp.concatenate(
            [
                mlp_gate[layer].reshape(strip, count, wide),
                mlp_up[layer].reshape(strip, count, wide),
            ],
            axis=2,
        ).transpose(1, 0, 2)
        in_weight = spread(in_pack).reshape(D, WIN + own)
        gate_rows = spread(gate_pack)
        blocks = gate_rows.transpose(1, 2, 0, 3, 4).reshape(2, 2, BW, BW)
        empty = jnp.zeros((BW, BW), jnp.bfloat16)
        gate_weights = []
        for which in range(2):
            whole = jnp.concatenate(
                [
                    jnp.concatenate([blocks[which, 0], empty], axis=1),
                    jnp.concatenate([empty, blocks[which, 1]], axis=1),
                ],
                axis=0,
            )
            gate_weights.append(turned(turned(whole, 0, shift), 1, shift)[:, :own])
        taps = jnp.concatenate(
            [
                small_all[:, layer, 2 * strip :].reshape(count, CONV + 1, own),
            ],
            axis=0,
        )
        taps = taps.transpose(1, 0, 2).reshape(CONV + 1, R)
        taps = lax.dynamic_slice_in_dim(taps, BW * first_block, WIN, 1)
        taps = high(turned(taps, 1, shift))
        weights.append(
            {
                "in": in_weight,
                "gates": jnp.concatenate(gate_weights, axis=1),
                "out": rec_out[layer],
                "taps": taps[:CONV],
                "bias": taps[CONV],
                "rate_bias": high(rate_bias[layer]),
                "input_bias": high(input_bias[layer]),
                "decay": high(decay_param[layer]),
                "norm_rec": high(small_whole(layer, 0, strip)),
                "norm_mlp": high(small_whole(layer, strip, strip)),
                "mlp": spread(mlp_pack).reshape(D, 2 * wide),
                "down": mlp_down[layer],
            }
        )

    keep = (1 - resets).astype(jnp.float32)
    padded = jnp.concatenate(
        [
            jnp.ones((MICRO, MARGIN), jnp.float32),
            keep,
            jnp.zeros((MICRO, length), jnp.float32),
        ],
        axis=1,
    )
    reach = 2 * MARGIN
    window = jnp.concatenate(
        [
            padded[:, :seq].reshape(MICRO, count, planes, length),
            padded[:, length : length + seq].reshape(MICRO, count, planes, length)[..., :reach],
        ],
        axis=3,
    )
    window = lax.dynamic_index_in_dim(window, rank, 2, keepdims=False)
    same = (devices[:, None] == jnp.arange(count)[None, :]).astype(jnp.float32)
    window = jnp.einsum("pj,mjr->pmr", same, window, precision=lax.Precision.HIGHEST)
    window = window.reshape(segments, length + reach)
    usable = [jnp.ones((segments, length + MARGIN, 1), jnp.float32)]
    for lag in range(1, CONV):
        begin = MARGIN - lag + 1
        usable.append(usable[-1] * window[:, begin : begin + length + MARGIN, None])
    carry_mask = window[:, MARGIN : MARGIN + length, None]

    edge_from = {}
    for step, plane in ((1, 0), (-1, planes - 1)):
        wanted = devices - jnp.where(rank == plane, step, 0)
        edge_from[step] = (wanted[:, None] == devices[None, :]).astype(jnp.float32)

    def edge(rows_out, step):
        came = lax.ppermute(
            rows_out, "section", [(at, (at + step) % planes) for at in range(planes)]
        )
        flat = came.reshape(count, -1)
        chosen = edge_from[step]
        moved = sum(chosen[:, q : q + 1] * flat[q][None] for q in range(count))
        return moved.reshape(rows_out.shape)

    def lru_parts(weight):
        rate = RATE_SCALE * jax.nn.softplus(-weight["decay"])
        return rate

    def rec_forward(section_in, weight):
        normed = low(rms_scale(high(section_in), weight["norm_rec"]))
        normed = gather_rows(normed)
        both = dot(normed, weight["in"])
        branch = both[:, :WIN].reshape(segments, length, WIN)
        side = both[:, WIN:].reshape(segments, length, own)
        extended = jnp.concatenate([edge(branch[:, length - MARGIN :], 1), branch], axis=1)
        conved = weight["bias"] + weight["taps"][0] * branch
        for lag in range(1, CONV):
            conved = (
                conved
                + weight["taps"][lag]
                * usable[lag][:, :length]
                * extended[:, MARGIN - lag : MARGIN - lag + length]
            )
        conv_low = low(conved).reshape(tokens, WIN)
        raw = dot(conv_low, weight["gates"])
        rate_sig = jax.nn.sigmoid(raw[:, :own] + weight["rate_bias"])
        input_sig = jax.nn.sigmoid(raw[:, own:] + weight["input_bias"])
        rate_sig = rate_sig.reshape(segments, length, own)
        input_sig = input_sig.reshape(segments, length, own)
        conved = conved[:, :, :own]
        decays = jnp.exp(-lru_parts(weight) * rate_sig) * carry_mask
        root = jnp.sqrt(1.0 + LRU_EPS - decays * decays)
        drives = root * input_sig * conved
        shape = (segments, length, own)
        cumulative, partial = in_vmem(forward_scan_kernel, [shape, shape], decays, drives)
        carry = carried(jnp.stack([cumulative[:, -1], partial[:, -1]]), False)
        states = partial + cumulative * carry[:, None]
        mixture = low(gelu_product(states, side)).reshape(tokens, own)
        result = high(section_in) + scatter_product(
            lambda left: dot(left, weight["out"]), mixture
        )
        kept = {
            "section_in": section_in,
            "normed": normed,
            "extended": extended,
            "side": side,
            "conved": conved,
            "conv_low": conv_low,
            "rate_sig": rate_sig,
            "input_sig": input_sig,
            "decays": decays,
            "root": root,
            "carry": carry,
            "states": states,
            "mixture": mixture,
        }
        return low(result), kept

    def mlp_forward(section_in, weight):
        normed = low(rms_scale(high(section_in), weight["norm_mlp"]))
        normed = gather_rows(normed)
        both = dot(normed, weight["mlp"])
        gate_val, up_val = both[:, :wide], both[:, wide:]
        hidden = low(gated_gelu(gate_val, up_val))
        result = high(section_in) + scatter_product(
            lambda left: dot(left, weight["down"]), hidden
        )
        kept = {
            "section_in": section_in,
            "normed": normed,
            "gate_val": gate_val,
            "up_val": up_val,
            "hidden": hidden,
        }
        return low(result), kept

    def mlp_backward(grad, weight, kept):
        grad_all = gather_rows(grad)
        grad_hidden = dot_nt(grad_all, weight["down"])
        _, pull = jax.vjp(gated_gelu, kept["gate_val"], kept["up_val"])
        gate_grad, up_grad = pull(grad_hidden)
        both = low(jnp.concatenate([gate_grad, up_grad], axis=1))
        grad_normed = scatter_product(lambda left: dot_nt(left, weight["mlp"]), both)
        _, pull = jax.vjp(rms_scale, high(kept["section_in"]), weight["norm_mlp"])
        grad_in, norm_grad = pull(grad_normed)
        terms = {
            "mlp": dot_tn(kept["normed"], both),
            "down": dot_tn(kept["hidden"], grad_all),
            "norm_mlp": norm_grad,
        }
        return low(grad_in + high(grad)), terms

    def rec_backward(grad, weight, kept):
        grad_all = gather_rows(grad)
        shape = (segments, length, own)
        grad_mixture = dot_nt(grad_all, weight["out"]).reshape(shape)
        _, pull = jax.vjp(gelu_product, kept["states"], kept["side"])
        grad_states0, grad_side = pull(grad_mixture)
        decays, root = kept["decays"], kept["root"]
        reached, partial, top = in_vmem(
            backward_scan_kernel,
            [shape, shape, (2, segments, own)],
            decays,
            grad_states0,
        )
        carry = carried(top, True)
        grad_states = partial + reached * carry[:, None]
        previous = jnp.concatenate([kept["carry"][:, None], kept["states"][:, :-1]], axis=1)
        conved, rate_sig, input_sig = kept["conved"], kept["rate_sig"], kept["input_sig"]
        grad_decays = grad_states * (previous - input_sig * conved * decays / root)
        slope = grad_decays * decays * rate_sig
        rate_grad = slope * (-lru_parts(weight)) * (1.0 - rate_sig)
        input_grad = grad_states * root * conved * input_sig * (1.0 - input_sig)
        raw_grad = low(
            jnp.concatenate([rate_grad, input_grad], axis=2).reshape(tokens, 2 * own)
        )
        spare = jnp.zeros((segments, length, WIN - own), jnp.float32)
        conv_grad = jnp.concatenate([grad_states * root * input_sig, spare], axis=2)
        conv_grad = conv_grad + dot_nt(raw_grad, weight["gates"]).reshape(segments, length, WIN)
        longer = jnp.concatenate([conv_grad, edge(conv_grad[:, :MARGIN], -1)], axis=1)
        branch_grad = weight["taps"][0] * conv_grad
        taps_grad = [jnp.sum(kept["extended"][:, MARGIN:] * conv_grad, axis=(0, 1))]
        for lag in range(1, CONV):
            branch_grad = (
                branch_grad
                + weight["taps"][lag]
                * usable[lag][:, lag : lag + length]
                * longer[:, lag : lag + length]
            )
            taps_grad.append(
                jnp.sum(
                    usable[lag][:, :length]
                    * kept["extended"][:, MARGIN - lag : MARGIN - lag + length]
                    * conv_grad,
                    axis=(0, 1),
                )
            )
        both = low(
            jnp.concatenate([branch_grad, grad_side], axis=2).reshape(tokens, WIN + own)
        )
        grad_normed = scatter_product(lambda left: dot_nt(left, weight["in"]), both)
        _, pull = jax.vjp(rms_scale, high(kept["section_in"]), weight["norm_rec"])
        grad_in, norm_grad = pull(grad_normed)
        terms = {
            "in": dot_tn(kept["normed"], both),
            "out": dot_tn(kept["mixture"], grad_all),
            "gates": dot_tn(kept["conv_low"], raw_grad),
            "taps": jnp.stack(taps_grad + [jnp.sum(conv_grad, axis=(0, 1))]),
            "rate_bias": jnp.sum(rate_grad, axis=(0, 1)),
            "input_bias": jnp.sum(input_grad, axis=(0, 1)),
            "decay": jnp.sum(slope, axis=(0, 1)) * RATE_SCALE * jax.nn.sigmoid(-weight["decay"]),
            "norm_rec": norm_grad,
        }
        return low(grad_in + high(grad)), terms

    def planes_first(term):
        split = low(term).reshape(count, planes, thin, term.shape[1])
        return split.transpose(1, 0, 2, 3)

    def gathered(piece, axis=0):
        return lax.all_gather(piece, "section", axis=axis, tiled=True)

    def mlp_gradients(terms):
        mine = spread(low(section_sum(planes_first(terms["mlp"]))))
        mine = mine.transpose(1, 0, 2)
        gate = mine[:, :, :wide].reshape(thin, F)
        up = mine[:, :, wide:].reshape(thin, F)
        down = low(section_sum(low(terms["down"]).reshape(planes, wide // planes, D)))
        return high(gathered(gate)), high(gathered(up)), high(gathered(down))

    def rec_gradients(terms):
        mine = high(spread(low(section_sum(planes_first(terms["in"])))))
        gate = low(mine[:, :, WIN:]).transpose(1, 0, 2).reshape(thin, R)
        branch = mine[:, :, :own].transpose(1, 0, 2).reshape(thin, R)
        for device in range(count):
            begin, end, left, right = window_of(device, count)
            if right > end:
                piece = mine[device, :, own : own + right - end]
                branch = branch + jnp.pad(piece, ((0, 0), (end, R - right)))
            if begin > left:
                piece = mine[device, :, own + right - end : WIN]
                branch = branch + jnp.pad(piece, ((0, 0), (left, R - begin)))
        out = low(section_sum(low(terms["out"]).reshape(planes, own // planes, D)))
        rows_each = BW // count
        blocks = []
        for which in range(2):
            square = jnp.concatenate(
                [
                    terms["gates"][:, which * own : (which + 1) * own],
                    jnp.zeros((WIN, WIN - own), jnp.float32),
                ],
                axis=1,
            )
            square = turned(turned(square, 0, -shift), 1, -shift)
            blocks.append(jnp.stack([square[:BW, :BW], square[BW:, BW:]]))
        blocks = low(jnp.stack(blocks)).reshape(
            2, 2, count, planes, rows_each // planes, BW
        )
        blocks = spread(low(section_sum(blocks.transpose(3, 2, 0, 1, 4, 5))))
        totals = [0.0] * H
        for device in range(count):
            first = window_of(device, count)[2] // BW
            for at in range(2):
                totals[first + at] = totals[first + at] + high(blocks[device, :, at])
        gates = gathered(low(jnp.stack(totals, axis=1)), 2)
        return (
            high(gathered(low(branch))),
            high(gathered(gate)),
            high(gathered(out)),
            high(gates[0]),
            high(gates[1]),
        )

    def small_gradients(terms):
        taps = turned(terms["taps"], 1, -shift)
        taps = lax.dynamic_update_slice(
            jnp.zeros((CONV + 1, R), jnp.float32), taps, (0, BW * first_block)
        )
        owned = jnp.stack([terms["rate_bias"], terms["input_bias"], terms["decay"]])
        owned = lax.dynamic_update_slice(
            jnp.zeros((3, R), jnp.float32), owned, (0, own_begin)
        )
        channels = jnp.concatenate([taps, owned], axis=0)
        norms = jnp.stack([terms["norm_rec"], terms["norm_mlp"]])
        flat = jnp.concatenate([channels.reshape(-1), norms.reshape(-1)])
        flat = lax.psum(flat.reshape(-1, 128), ("section", "dp")).reshape(-1)
        channels = flat[: (CONV + 4) * R].reshape(CONV + 4, R)
        norms = flat[(CONV + 4) * R :].reshape(2, D)
        channels = lax.dynamic_slice_in_dim(channels, own_begin, own, 1)
        norms = lax.dynamic_slice_in_dim(norms, strip * me, strip, 1)
        return channels, norms

    def by_tokens(value):
        moved = lax.all_to_all(value, "section", split_axis=1, concat_axis=2, tiled=True)
        return moved.reshape(rows, D)

    def by_features(value):
        moved = value.reshape(MICRO, length, D)
        return lax.all_to_all(moved, "section", split_axis=2, concat_axis=1, tiled=True)

    stream = by_tokens(inputs)
    kept = []
    for layer in range(LAYERS):
        stream, kept_rec = rec_forward(stream, weights[layer])
        stream, kept_mlp = mlp_forward(stream, weights[layer])
        kept.append((kept_rec, kept_mlp))
    output = by_features(stream)
    grad = by_tokens(cotangent)
    results = [None] * LAYERS
    for layer in reversed(range(LAYERS)):
        grad, mlp_terms = mlp_backward(grad, weights[layer], kept[layer][1])
        mlp_grads = mlp_gradients(mlp_terms)
        grad, rec_terms = rec_backward(grad, weights[layer], kept[layer][0])
        rec_grads = rec_gradients(rec_terms)
        channels, norms = small_gradients({**mlp_terms, **rec_terms})
        results[layer] = rec_grads + (
            channels[:CONV],
            channels[CONV],
            channels[CONV + 1],
            channels[CONV + 2],
            channels[CONV + 3],
            norms[0],
            norms[1],
        ) + mlp_grads
    input_grad = by_features(grad)
    stacked = tuple(jnp.stack(parts) for parts in zip(*results))
    return (output, input_grad) + stacked


def solution(mesh):
    return jax.shard_map(
        local,
        mesh=mesh,
        in_specs=(
            P(None, "dp", "section"),
            P(None, "dp", "section"),
            P(),
            P(None, "dp", None),
            P(None, "dp", None),
            P(None, "dp", None),
            P(None, None, "dp", None),
            P(None, None, "dp", None),
            P(None, None, "dp"),
            P(None, "dp"),
            P(None, "dp"),
            P(None, "dp"),
            P(None, "dp"),
            P(None, "dp"),
            P(None, "dp"),
            P(None, "dp", None),
            P(None, "dp", None),
            P(None, "dp", None),
        ),
        out_specs=(
            P(None, "dp", "section"),
            P(None, "dp", "section"),
            P(None, "dp", None),
            P(None, "dp", None),
            P(None, "dp", None),
            P(None, None, "dp", None),
            P(None, None, "dp", None),
            P(None, None, "dp"),
            P(None, "dp"),
            P(None, "dp"),
            P(None, "dp"),
            P(None, "dp"),
            P(None, "dp"),
            P(None, "dp"),
            P(None, "dp", None),
            P(None, "dp", None),
            P(None, "dp", None),
        ),
        check_vma=False,
    )
```

```python
import jax
import jax.numpy as jnp
from jax import lax
from jax.experimental import pallas as pl
from jax.experimental.pallas import tpu as pltpu
from jax.sharding import PartitionSpec as P

D = 2048
H = 10
BW = 256
F = 6144
R = 2560
CONV = 4
MICRO = 2
LAYERS = 2
MARGIN = CONV - 1
WIN = 2 * BW

EPS = 1e-06
LRU_EPS = 0.04
RATE_SCALE = 8.0


def low(value):
    return value.astype(jnp.bfloat16)


def high(value):
    return value.astype(jnp.float32)


def dot(left, right):
    return jnp.dot(left, right, preferred_element_type=jnp.float32)


def dot_nt(left, right):
    return lax.dot_general(
        left, right, (((1,), (1,)), ((), ())), preferred_element_type=jnp.float32
    )


def dot_tn(left, right):
    return lax.dot_general(
        left, right, (((0,), (0,)), ((), ())), preferred_element_type=jnp.float32
    )


def rms_scale(values, scales):
    return values * lax.rsqrt(jnp.mean(values * values, axis=-1, keepdims=True) + EPS) * scales


def meeting_order(count):
    return list(range(0, count, 2)) + list(range(1, count, 2))


def swapped(value, offset):
    count = lax.axis_size("dp")
    return lax.ppermute(value, "dp", [(at, at ^ offset) for at in range(count)])


def gather_rows(block):
    count = lax.axis_size("dp")
    same_core = jnp.concatenate([block] + [swapped(block, k) for k in range(2, count, 2)], axis=0)
    other_core = swapped(same_core, 1)
    return jnp.concatenate([same_core, other_core], axis=0)


def scatter_product(product, left):
    count = lax.axis_size("dp")
    half = left.shape[0] // 2
    rows = left.shape[0] // count
    away = swapped(low(product(left[half:])), 1)
    here = product(left[:half]) + high(away)
    total = here[:rows]
    for k in range(2, count, 2):
        piece = here[(k // 2) * rows : (k // 2 + 1) * rows]
        total = total + high(swapped(low(piece), k))
    return total


def spread(pack):
    return lax.all_to_all(pack, "dp", 0, 0, tiled=False)


def section_sum(chunks):
    return lax.psum_scatter(chunks, "section", scatter_dimension=0, tiled=False)


def all_rows(block):
    return lax.all_gather(block, ("dp", "section"), axis=0, tiled=True)


def other_planes(value):
    count = lax.axis_size("section")
    return [
        lax.ppermute(value, "section", [(at, at ^ k) for at in range(count)])
        for k in range(1, count)
    ]


def columns_apart(first, second, layer, count):
    rows, columns = first.shape[1], first.shape[2] // count
    if columns % 128:
        parts = [
            part[layer].reshape(rows, count, columns).transpose(1, 0, 2)
            for part in (first, second)
        ]
        return jnp.concatenate(parts, axis=2)

    def kernel(first_ref, second_ref, out_ref):
        out_ref[0, :, :columns] = first_ref[0]
        out_ref[0, :, columns:] = second_ref[0]

    return pl.pallas_call(
        kernel,
        out_shape=jax.ShapeDtypeStruct((count, rows, 2 * columns), first.dtype),
        grid=(count,),
        in_specs=[pl.BlockSpec((1, rows, columns), lambda at: (layer, 0, at))] * 2,
        out_specs=pl.BlockSpec((1, rows, 2 * columns), lambda at: (at, 0, 0)),
        cost_estimate=pl.CostEstimate(
            flops=0, transcendentals=0, bytes_accessed=8 * count * rows * columns
        ),
        compiler_params=pltpu.CompilerParams(vmem_limit_bytes=16 * 1024 * 1024),
    )(first, second)


def packed_columns(branch, gate, blocks, layer, filler):
    count, rows, extra = blocks.shape
    own = R // count
    width = WIN + own + filler + extra
    if own % 64:
        packs = []
        for device in range(count):
            begin, end, left, right = window_of(device, count)
            packs.append(
                jnp.concatenate(
                    own_first(branch[layer], device, count)
                    + [gate[layer][:, begin:end]]
                    + [jnp.zeros((rows, filler), branch.dtype), blocks[device]],
                    axis=1,
                )
            )
        return jnp.stack(packs)

    def kernel(branch_ref, gate_ref, blocks_ref, out_ref):
        for device in range(count):
            begin, end, left, right = window_of(device, count)
            at = 0
            for ref, start, stop in (
                (branch_ref, begin, end),
                (branch_ref, end, right),
                (branch_ref, left, begin),
                (gate_ref, begin, end),
            ):
                if stop > start:
                    out_ref[device, :, at : at + stop - start] = ref[0, :, start:stop]
                    at += stop - start
            if filler:
                out_ref[device, :, at : at + filler] = jnp.zeros((rows, filler), out_ref.dtype)
            out_ref[device, :, at + filler :] = blocks_ref[device]

    whole = pl.BlockSpec((1, rows, R), lambda at: (layer, 0, 0))
    return pl.pallas_call(
        kernel,
        out_shape=jax.ShapeDtypeStruct((count, rows, width), branch.dtype),
        grid=(1,),
        in_specs=[whole, whole, pl.BlockSpec((count, rows, extra), lambda at: (0, 0, 0))],
        out_specs=pl.BlockSpec((count, rows, width), lambda at: (0, 0, 0)),
        cost_estimate=pl.CostEstimate(
            flops=0, transcendentals=0, bytes_accessed=4 * count * rows * width
        ),
        compiler_params=pltpu.CompilerParams(vmem_limit_bytes=40 * 1024 * 1024),
    )(branch, gate, blocks)


def rows_kernel(part_ref, kept_ref, out_ref):
    del kept_ref
    out_ref[0] = part_ref[0].astype(jnp.float32)


def first_rows_kernel(part_ref, out_ref):
    out_ref[0] = part_ref[0].astype(jnp.float32)


def joined_rows(part, which, layer, layers, out):
    count, rows, columns = part.shape[0], part.shape[1], part.shape[2] // 2
    if columns % 128:
        part = part[:, :, which * columns : (which + 1) * columns]
        whole = jnp.zeros((layers, rows, count * columns), jnp.float32) if out is None else out
        piece = high(part.transpose(1, 0, 2).reshape(1, rows, -1))
        return lax.dynamic_update_slice_in_dim(whole, piece, layer, 0)
    operands = [part] + ([] if out is None else [out])
    return pl.pallas_call(
        first_rows_kernel if out is None else rows_kernel,
        out_shape=jax.ShapeDtypeStruct((layers, rows, count * columns), jnp.float32),
        grid=(count,),
        in_specs=[pl.BlockSpec((1, rows, columns), lambda at: (at, 0, which))]
        + [pl.BlockSpec(memory_space=pl.ANY)] * (len(operands) - 1),
        out_specs=pl.BlockSpec((1, rows, columns), lambda at: (layer, 0, at)),
        input_output_aliases={1: 0} if len(operands) > 1 else {},
        cost_estimate=pl.CostEstimate(
            flops=0, transcendentals=0, bytes_accessed=6 * count * rows * columns
        ),
        compiler_params=pltpu.CompilerParams(vmem_limit_bytes=16 * 1024 * 1024),
    )(*operands)


def after(value, *others):
    return lax.optimization_barrier((value,) + others)


def after_all(values, *others):
    return lax.optimization_barrier(tuple(values) + others)[: len(values)]


def lane_blocks(value, width):
    rows, columns = value.shape[-2:]
    split = value.reshape(value.shape[:-1] + (columns // width, width))
    return jnp.swapaxes(split, -3, -2).reshape(value.shape[:-2] + (-1, width))


def whole_rows(value, rows):
    blocks = value.shape[-2] // rows
    split = value.reshape(value.shape[:-2] + (blocks, rows, value.shape[-1]))
    return jnp.swapaxes(split, -3, -2).reshape(value.shape[:-2] + (rows, -1))


def window_of(device, count):
    own = R // count
    first_block = min(own * device // BW, H - 2)
    return own * device, own * (device + 1), BW * first_block, BW * first_block + WIN


def own_first(matrix, device, count):
    begin, end, left, right = window_of(device, count)
    return [matrix[:, begin:end], matrix[:, end:right], matrix[:, left:begin]]


def turned(value, axis, shift):
    size = value.shape[axis]
    twice = jnp.concatenate([value, value], axis=axis)
    return lax.dynamic_slice_in_dim(twice, jnp.mod(shift, size), size, axis)


def forward_scan_kernel(decay_ref, drive_ref, reach_ref, state_ref):
    rows = decay_ref.shape[1]
    reach = decay_ref[:, 0, :]
    state = drive_ref[:, 0, :]
    reach_ref[:, 0, :] = reach
    state_ref[:, 0, :] = state
    for row in range(1, rows):
        decay = decay_ref[:, row, :]
        state = decay * state + drive_ref[:, row, :]
        reach = decay * reach
        reach_ref[:, row, :] = reach
        state_ref[:, row, :] = state


def backward_scan_kernel(decay_ref, grad_ref, reach_ref, local_ref, top_ref):
    rows = decay_ref.shape[1]
    reach = jnp.ones_like(decay_ref[:, 0, :])
    local = grad_ref[:, rows - 1, :]
    reach_ref[:, rows - 1, :] = reach
    local_ref[:, rows - 1, :] = local
    for row in range(rows - 2, -1, -1):
        decay = decay_ref[:, row + 1, :]
        local = decay * local + grad_ref[:, row, :]
        reach = decay * reach
        reach_ref[:, row, :] = reach
        local_ref[:, row, :] = local
    top_ref[0] = decay_ref[:, 0, :] * reach
    top_ref[1] = decay_ref[:, 0, :] * local


def carry_kernel(reverse, where_ref, totals_ref, carry_ref):
    planes, count = totals_ref.shape[0], totals_ref.shape[2]
    me, rank = where_ref[0], where_ref[1]
    state = jnp.zeros(carry_ref.shape[1:], jnp.float32)
    for step in range(count):
        device = count - 1 - step if reverse else step
        offset = jnp.bitwise_xor(me, device)
        at = offset // 2 + (offset % 2) * (count // 2)
        for plane in range(planes - 1, -1, -1) if reverse else range(planes):

            @pl.when(rank == plane)
            def _(state=state, at=at):
                carry_ref[at] = state

            met = jnp.bitwise_xor(rank, plane)
            state = totals_ref[met, 0, at] * state + totals_ref[met, 1, at]


VMEM_SPEC = pl.BlockSpec(memory_space=pltpu.VMEM)


def in_vmem(kernel, shapes, *operands, scalars=0):
    specs = [pl.BlockSpec(memory_space=pltpu.SMEM)] * scalars
    return pl.pallas_call(
        kernel,
        out_shape=tuple(jax.ShapeDtypeStruct(shape, jnp.float32) for shape in shapes),
        in_specs=specs + [VMEM_SPEC] * (len(operands) - scalars),
        out_specs=tuple(VMEM_SPEC for _ in shapes),
        compiler_params=pltpu.CompilerParams(vmem_limit_bytes=40 * 1024 * 1024),
    )(*operands)


def carried(totals, reverse):
    count = lax.axis_size("dp")
    channels = totals.shape[-1]
    totals = totals.reshape(2, count, MICRO, channels)
    everything = jnp.stack([totals] + other_planes(totals))
    where = jnp.stack([lax.axis_index("dp"), lax.axis_index("section")]).astype(jnp.int32)

    def kernel(where_ref, totals_ref, carry_ref):
        carry_kernel(reverse, where_ref, totals_ref, carry_ref)

    (carry,) = in_vmem(kernel, [(count, MICRO, channels)], where, everything, scalars=1)
    return carry.reshape(count * MICRO, channels)


def gelu_product(states, side):
    return states * jax.nn.gelu(side)


def gated_gelu(gate_val, up_val):
    return jax.nn.gelu(gate_val) * up_val


def local(
    inputs,
    cotangent,
    resets,
    branch_in,
    gate_in,
    rec_out,
    rate_gate,
    input_gate,
    conv_taps,
    conv_bias,
    rate_bias,
    input_bias,
    decay_param,
    norm_rec,
    norm_mlp,
    mlp_gate,
    mlp_up,
    mlp_down,
):
    planes = lax.axis_size("section")
    count = lax.axis_size("dp")
    rank = lax.axis_index("section")
    me = lax.axis_index("dp")
    block_rows = inputs.shape[1]
    length = block_rows // planes
    seq = resets.shape[1]
    rows = MICRO * length
    segments = MICRO * count
    tokens = segments * length
    own = R // count
    wide = F // count
    strip = D // count
    thin = strip // planes
    filler = D // 2 - BW // 2 - WIN - own
    order = jnp.array(meeting_order(count), jnp.int32)
    devices = jnp.bitwise_xor(me, order)

    small = jnp.concatenate(
        [
            norm_rec,
            norm_mlp,
            conv_taps.reshape(LAYERS, CONV * own),
            conv_bias,
        ],
        axis=1,
    )
    small_all = lax.all_gather(small, "dp", axis=0, tiled=False)
    own_begin = own * me
    first_block = jnp.minimum(own_begin // BW, H - 2)
    shift = own_begin - BW * first_block

    def small_whole(layer, begin, each):
        return small_all[:, layer, begin : begin + each].reshape(count * each)

    def packed_in(layer, shared):
        def cut(value, axis):
            if not shared:
                return value
            size = value.shape[axis] // planes
            return lax.dynamic_slice_in_dim(value, size * rank, size, axis)

        gates = cut(jnp.stack([rate_gate[layer], input_gate[layer]]), 2)
        blocks = []
        for device in range(count):
            begin, end, left, right = window_of(device, count)
            height = thin if shared else strip
            blocks.append(gates[:, left // BW : right // BW].reshape(height, -1))
        branch, gate, at = branch_in, gate_in, layer
        if shared:
            branch, gate, at = cut(branch_in[layer:], 1), cut(gate_in[layer:], 1), 0
        return packed_columns(branch, gate, jnp.stack(blocks), at, filler)

    def by_features(value):
        moved = value.reshape(MICRO, length, D)
        return lax.all_to_all(moved, "section", split_axis=2, concat_axis=1, tiled=True)

    both_ends = lax.all_to_all(
        jnp.concatenate([inputs, cotangent], axis=0), "section", 1, 2, tiled=True
    )
    stream, grad = both_ends[:MICRO].reshape(rows, D), both_ends[MICRO:].reshape(rows, D)
    top_grad_all = all_rows(grad)
    in_moved = [None] * LAYERS
    mlp_moved = [None] * LAYERS
    in_moved[0] = spread(after(packed_in(0, False), small_all, stream)[0])
    normed = low(rms_scale(high(stream), high(small_whole(0, 0, strip))))
    first_normed = gather_rows(normed)
    in_width = WIN + own + filler
    first_both = dot(first_normed, in_moved[0].reshape(D, -1)[:, :in_width])
    mlp_moved[0] = spread(after(columns_apart(mlp_gate, mlp_up, 0, count), first_both)[0])
    def layer_weights(layer):
        in_weight = in_moved[layer].reshape(D, -1)
        blocks = in_weight[:, WIN + own + filler :]
        parts = planes if layer else 1
        blocks = blocks.reshape(count, parts, 2, 2, BW // count // parts, BW)
        blocks = blocks.transpose(2, 3, 0, 1, 4, 5).reshape(2, 2, BW, BW)
        in_weight = in_weight[:, : WIN + own + filler]
        empty = jnp.zeros((BW, BW), jnp.bfloat16)
        gate_weights = []
        for which in range(2):
            whole = jnp.concatenate(
                [
                    jnp.concatenate([blocks[which, 0], empty], axis=1),
                    jnp.concatenate([empty, blocks[which, 1]], axis=1),
                ],
                axis=0,
            )
            gate_weights.append(turned(turned(whole, 0, shift), 1, shift)[:, :own])
        taps = jnp.concatenate(
            [
                small_all[:, layer, 2 * strip :].reshape(count, CONV + 1, own),
            ],
            axis=0,
        )
        taps = taps.transpose(1, 0, 2).reshape(CONV + 1, R)
        taps = lax.dynamic_slice_in_dim(taps, BW * first_block, WIN, 1)
        taps = high(turned(taps, 1, shift))
        return (
            {
                "in": in_weight,
                "gates": jnp.concatenate(gate_weights, axis=1),
                "out": rec_out[layer],
                "taps": taps[:CONV],
                "bias": taps[CONV],
                "rate_bias": high(rate_bias[layer]),
                "input_bias": high(input_bias[layer]),
                "decay": high(decay_param[layer]),
                "norm_rec": high(small_whole(layer, 0, strip)),
                "norm_mlp": high(small_whole(layer, strip, strip)),
                "down": mlp_down[layer],
            }
        )

    keep = (1 - resets).astype(jnp.float32)
    padded = jnp.concatenate(
        [
            jnp.ones((MICRO, MARGIN), jnp.float32),
            keep,
            jnp.zeros((MICRO, length), jnp.float32),
        ],
        axis=1,
    )
    reach = 2 * MARGIN
    window = jnp.concatenate(
        [
            padded[:, :seq].reshape(MICRO, count, planes, length),
            padded[:, length : length + seq].reshape(MICRO, count, planes, length)[..., :reach],
        ],
        axis=3,
    )
    window = lax.dynamic_index_in_dim(window, rank, 2, keepdims=False)
    same = (devices[:, None] == jnp.arange(count)[None, :]).astype(jnp.float32)
    window = jnp.einsum("pj,mjr->pmr", same, window, precision=lax.Precision.HIGHEST)
    window = window.reshape(segments, length + reach)
    usable = [jnp.ones((segments, length + MARGIN, 1), jnp.float32)]
    for lag in range(1, CONV):
        begin = MARGIN - lag + 1
        usable.append(usable[-1] * window[:, begin : begin + length + MARGIN, None])
    carry_mask = window[:, MARGIN : MARGIN + length, None]

    edge_from = {}
    for step, plane in ((1, 0), (-1, planes - 1)):
        wanted = devices - jnp.where(rank == plane, step, 0)
        edge_from[step] = (wanted[:, None] == devices[None, :]).astype(jnp.float32)

    def edge(rows_out, step):
        came = lax.ppermute(
            rows_out, "section", [(at, (at + step) % planes) for at in range(planes)]
        )
        flat = came.reshape(count, -1)
        chosen = edge_from[step]
        moved = sum(chosen[:, q : q + 1] * flat[q][None] for q in range(count))
        return moved.reshape(rows_out.shape)

    def lru_parts(weight):
        rate = RATE_SCALE * jax.nn.softplus(-weight["decay"])
        return rate

    def rec_forward(section_in, weight, normed, both, late):
        if normed is None:
            normed = gather_rows(low(rms_scale(high(section_in), weight["norm_rec"])))
            both = dot(normed, weight["in"])
        branch = both[:, :WIN].reshape(segments, length, WIN)
        side = both[:, WIN : WIN + own].reshape(segments, length, own)
        extended = jnp.concatenate([edge(branch[:, length - MARGIN :], 1), branch], axis=1)
        conved = weight["bias"] + weight["taps"][0] * branch
        for lag in range(1, CONV):
            conved = (
                conved
                + weight["taps"][lag]
                * usable[lag][:, :length]
                * extended[:, MARGIN - lag : MARGIN - lag + length]
            )
        conv_low = low(conved).reshape(tokens, WIN)
        raw = dot(conv_low, weight["gates"])
        rate_sig = jax.nn.sigmoid(raw[:, :own] + weight["rate_bias"])
        input_sig = jax.nn.sigmoid(raw[:, own:] + weight["input_bias"])
        rate_sig = rate_sig.reshape(segments, length, own)
        input_sig = input_sig.reshape(segments, length, own)
        conved = conved[:, :, :own]
        decays = jnp.exp(-lru_parts(weight) * rate_sig) * carry_mask
        root = jnp.sqrt(1.0 + LRU_EPS - decays * decays)
        drives = root * input_sig * conved
        shape = (segments, length, own)
        cumulative, partial = in_vmem(forward_scan_kernel, [shape, shape], decays, drives)
        carry = carried(jnp.stack([cumulative[:, -1], partial[:, -1]]), False)
        states = partial + cumulative * carry[:, None]
        mixture = low(gelu_product(states, side)).reshape(tokens, own)
        mixture = after(mixture, *late)[0]
        result = high(section_in) + scatter_product(
            lambda left: dot(left, weight["out"]), mixture
        )
        kept = {
            "section_in": section_in,
            "normed": normed,
            "extended": extended,
            "side": side,
            "conved": conved,
            "conv_low": conv_low,
            "rate_sig": rate_sig,
            "input_sig": input_sig,
            "decays": decays,
            "root": root,
            "carry": carry,
            "states": states,
            "mixture": mixture,
        }
        return low(result), kept

    def mlp_forward(section_in, weight, late):
        normed = low(rms_scale(high(section_in), weight["norm_mlp"]))
        here = normed
        normed = gather_rows(normed)
        both = dot(normed, weight["mlp"])
        gate_val, up_val = both[:, :wide], both[:, wide:]
        hidden = after(low(gated_gelu(gate_val, up_val)), *late)[0]
        result = high(section_in) + scatter_product(
            lambda left: dot(left, weight["down"]), hidden
        )
        kept = {
            "section_in": section_in,
            "normed": here,
            "hidden": hidden,
            "gate_val": gate_val,
            "up_val": up_val,
        }
        return low(result), kept

    def mlp_backward(grad, weight, kept):
        grad_all = gather_rows(grad)
        grad_hidden = dot_nt(grad_all, weight["down"])
        _, pull = jax.vjp(gated_gelu, kept["gate_val"], kept["up_val"])
        gate_grad, up_grad = pull(grad_hidden)
        both = jnp.concatenate([low(gate_grad), low(up_grad)], axis=1)
        grad_normed = scatter_product(lambda left: dot_nt(left, weight["mlp"]), both)
        _, pull = jax.vjp(rms_scale, high(kept["section_in"]), weight["norm_mlp"])
        grad_in, norm_grad = pull(grad_normed)
        return low(grad_in + high(grad)), {"norm_mlp": norm_grad}

    def rec_backward(grad, weight, kept, early):
        grad_all = gather_rows(grad)
        shape = (segments, length, own)
        grad_mixture = dot_nt(grad_all, weight["out"]).reshape(shape)
        _, pull = jax.vjp(gelu_product, kept["states"], kept["side"])
        grad_states0, grad_side = pull(grad_mixture)
        decays, root = kept["decays"], kept["root"]
        reached, partial, top = in_vmem(
            backward_scan_kernel,
            [shape, shape, (2, segments, own)],
            decays,
            grad_states0,
        )
        carry = carried(after(top, *early)[0], True)
        grad_states = partial + reached * carry[:, None]
        previous = jnp.concatenate([kept["carry"][:, None], kept["states"][:, :-1]], axis=1)
        conved, rate_sig, input_sig = kept["conved"], kept["rate_sig"], kept["input_sig"]
        grad_decays = grad_states * (previous - input_sig * conved * decays / root)
        slope = grad_decays * decays * rate_sig
        rate_grad = slope * (-lru_parts(weight)) * (1.0 - rate_sig)
        input_grad = grad_states * root * conved * input_sig * (1.0 - input_sig)
        raw_grad = low(
            jnp.concatenate([rate_grad, input_grad], axis=2).reshape(tokens, 2 * own)
        )
        spare = jnp.zeros((segments, length, WIN - own), jnp.float32)
        conv_grad = jnp.concatenate([grad_states * root * input_sig, spare], axis=2)
        conv_grad = conv_grad + dot_nt(raw_grad, weight["gates"]).reshape(segments, length, WIN)
        longer = jnp.concatenate([conv_grad, edge(conv_grad[:, :MARGIN], -1)], axis=1)
        branch_grad = weight["taps"][0] * conv_grad
        taps_grad = [jnp.sum(kept["extended"][:, MARGIN:] * conv_grad, axis=(0, 1))]
        for lag in range(1, CONV):
            branch_grad = (
                branch_grad
                + weight["taps"][lag]
                * usable[lag][:, lag : lag + length]
                * longer[:, lag : lag + length]
            )
            taps_grad.append(
                jnp.sum(
                    usable[lag][:, :length]
                    * kept["extended"][:, MARGIN - lag : MARGIN - lag + length]
                    * conv_grad,
                    axis=(0, 1),
                )
            )
        both = low(
            jnp.concatenate(
                [branch_grad, grad_side, jnp.zeros((segments, length, filler), jnp.float32)],
                axis=2,
            ).reshape(tokens, WIN + own + filler)
        )
        grad_normed = scatter_product(lambda left: dot_nt(left, weight["in"]), both)
        _, pull = jax.vjp(rms_scale, high(kept["section_in"]), weight["norm_rec"])
        grad_in, norm_grad = pull(grad_normed)
        terms = {
            "in": dot_tn(kept["normed"], both),
            "out": dot_tn(kept["mixture"], grad_all),
            "gates": dot_tn(kept["conv_low"], raw_grad),
            "taps": jnp.stack(taps_grad + [jnp.sum(conv_grad, axis=(0, 1))]),
            "rate_bias": jnp.sum(rate_grad, axis=(0, 1)),
            "input_bias": jnp.sum(input_grad, axis=(0, 1)),
            "decay": jnp.sum(slope, axis=(0, 1)) * RATE_SCALE * jax.nn.sigmoid(-weight["decay"]),
            "norm_rec": norm_grad,
            "in_grads": both,
        }
        return low(grad_in + high(grad)), terms

    def mlp_gradients(normed, grad_all, weight):
        both = dot(normed, weight["mlp"])
        product, pull = jax.vjp(gated_gelu, both[:, :wide], both[:, wide:])
        gate_grad, up_grad = pull(dot_nt(grad_all, weight["down"]))
        both_grad = jnp.concatenate([low(gate_grad), low(up_grad)], axis=1)
        return low(dot_tn(normed, both_grad)), dot_tn(low(product), grad_all)

    def to_rows(part):
        return spread(part.reshape(count, strip, 2 * wide))

    def rec_shares(terms):
        each = BW // count // planes
        blocks = []
        for which in range(2):
            square = jnp.concatenate(
                [
                    terms["gates"][:, which * own : (which + 1) * own],
                    jnp.zeros((WIN, WIN - own), jnp.float32),
                ],
                axis=1,
            )
            square = turned(turned(square, 0, -shift), 1, -shift)
            blocks.append(jnp.stack([square[:BW, :BW], square[BW:, BW:]]))
        blocks = low(jnp.stack(blocks)).reshape(2, 2, count, planes, each, 2, BW // 2)
        blocks = blocks.transpose(3, 2, 0, 1, 4, 5, 6).reshape(planes, count, 8 * each, BW // 2)
        blocks = blocks.reshape(planes, count, thin, -1)
        mixed = low(terms["in"]).reshape(count, planes, thin, WIN + own + filler)
        mixed = jnp.concatenate([mixed.transpose(1, 0, 2, 3), blocks], axis=3)
        width = mixed.shape[-1]
        out = low(terms["out"]).reshape(planes, own // planes, D)
        flat = jnp.concatenate(
            [mixed.reshape(planes, count * thin, width), lane_blocks(out, width)], axis=1
        )
        return flat

    def rec_pieces(flat):
        each = BW // count // planes
        width = WIN + own + filler + 8 * each * (BW // 2) // thin
        out = whole_rows(flat[count * thin :], own // planes)
        mine = spread(flat[: count * thin].reshape(count, thin, width))
        blocks = mine[:, :, WIN + own + filler :].reshape(count, 2, 2, each, BW)
        mine = high(mine)
        gate = low(mine[:, :, WIN : WIN + own]).transpose(1, 0, 2).reshape(thin, R)
        branch = mine[:, :, :own].transpose(1, 0, 2).reshape(thin, R)
        for device in range(count):
            begin, end, left, right = window_of(device, count)
            if right > end:
                piece = mine[device, :, own : own + right - end]
                branch = branch + jnp.pad(piece, ((0, 0), (end, R - right)))
            if begin > left:
                piece = mine[device, :, own + right - end : WIN]
                branch = branch + jnp.pad(piece, ((0, 0), (left, R - begin)))
        totals = [0.0] * H
        for device in range(count):
            first = window_of(device, count)[2] // BW
            for at in range(2):
                totals[first + at] = totals[first + at] + high(blocks[device, :, at])
        gates = low(jnp.stack(totals, axis=1))
        return jnp.concatenate(
            [
                lane_blocks(low(branch), WIN),
                lane_blocks(gate, WIN),
                lane_blocks(out, WIN),
                lane_blocks(gates.reshape(-1, 2 * BW), WIN),
            ],
            axis=0,
        )

    def rec_gradients(flat):
        each = BW // count // planes
        sizes = [thin * R // WIN, thin * R // WIN, own // planes * D // WIN]
        at = [0, sizes[0], sizes[0] + sizes[1], sum(sizes)]
        branch = whole_rows(flat[:, at[0] : at[1]], thin).reshape(strip, R)
        gate = whole_rows(flat[:, at[1] : at[2]], thin).reshape(strip, R)
        out = whole_rows(flat[:, at[2] : at[3]], own // planes).reshape(own, D)
        gates = flat[:, at[3] :].reshape(planes, 2, H, each, BW)
        gates = gates.transpose(1, 2, 0, 3, 4).reshape(2, H, BW // count, BW)
        return branch, gate, out, gates[0], gates[1]

    def small_gradients(terms):
        taps = turned(terms["taps"], 1, -shift)
        taps = lax.dynamic_update_slice(
            jnp.zeros((CONV + 1, R), jnp.float32), taps, (0, BW * first_block)
        )
        owned = jnp.stack([terms["rate_bias"], terms["input_bias"], terms["decay"]])
        owned = lax.dynamic_update_slice(
            jnp.zeros((3, R), jnp.float32), owned, (0, own_begin)
        )
        channels = jnp.concatenate([taps, owned], axis=0)
        norms = jnp.stack([terms["norm_rec"], terms["norm_mlp"]])
        pack = jnp.concatenate(
            [
                channels.reshape(CONV + 4, count, own).transpose(1, 0, 2).reshape(count, -1),
                norms.reshape(2, count, strip).transpose(1, 0, 2).reshape(count, -1),
            ],
            axis=1,
        )
        mine = jnp.sum(spread(pack), axis=0)
        mine = mine.reshape(-1, 128)
        mine = (mine + sum(other_planes(mine))).reshape(-1)
        channels = mine[: (CONV + 4) * own].reshape(CONV + 4, own)
        norms = mine[(CONV + 4) * own :].reshape(2, strip)
        return channels, norms

    weights = [layer_weights(0)]
    weights[0]["mlp"] = mlp_moved[0].reshape(D, 2 * wide)
    kept = []
    everyone = [None] * LAYERS
    top = LAYERS - 1
    for layer in range(LAYERS):
        weight = weights[layer]
        first = layer == 0
        stream, kept_rec = rec_forward(
            stream,
            weight,
            first_normed if first else None,
            first_both if first else None,
            [weight["mlp"], top_grad_all] if first else [],
        )
        if first:
            in_share = spread(after(packed_in(1, True), kept_rec["mixture"])[0])
            in_moved[1] = lax.all_gather(in_share, "section", axis=1, tiled=True)
            shares = [
                lax.dynamic_slice_in_dim(part[1:], thin * rank, thin, 1)
                for part in (mlp_gate, mlp_up)
            ]
            share = spread(after(columns_apart(*shares, 0, count), in_share)[0])
            share = after(share, in_moved[1])[0]
            mlp_moved[1] = lax.all_gather(share, "section", axis=1, tiled=True)
            weights.append(layer_weights(1))
        else:
            everyone[0] = all_rows(after(kept[0][1]["normed"], kept_rec["mixture"])[0])
        stream, kept_mlp = mlp_forward(stream, weight, [in_share] if first else [])
        if first:
            weights[1]["mlp"] = mlp_moved[1].reshape(D, 2 * wide)
        else:
            everyone[1] = all_rows(after(kept_mlp["normed"], stream)[0])
        kept.append((kept_rec, kept_mlp))
    output = by_features(stream)
    mlp_downs = [None] * LAYERS
    mlp_rows = [None] * LAYERS
    rec_flat = [None] * LAYERS
    smalls = [None] * LAYERS

    grad_in = grad
    grad, mlp_terms = mlp_backward(grad_in, weights[1], kept[1][1])
    ins1, mlp_downs[1] = mlp_gradients(everyone[1], top_grad_all, weights[1])
    grad, everyone[0] = after(grad, everyone[0])
    grad, terms = rec_backward(grad, weights[1], kept[1][0], [output])
    grad, everyone[1] = after(grad, everyone[1])
    flat = section_sum(rec_shares(terms))
    smalls[1] = small_gradients({**mlp_terms, **terms})
    mlp_rows[1] = to_rows(ins1)

    grad_in = grad
    grad_mid, mlp_terms = mlp_backward(grad_in, weights[0], kept[0][1])
    pieces1 = rec_pieces(after(flat, grad_mid)[0])
    rec_flat[1] = lax.all_gather(pieces1, "section", axis=0, tiled=False)
    grad_all = all_rows(grad_in)
    grad, terms = rec_backward(grad_mid, weights[0], kept[0][0], [pieces1, ins1])
    input_grad = by_features(grad)
    flat = rec_shares(terms)
    grad_all = after(grad_all, flat)[0]
    flat = section_sum(flat)
    smalls[0] = small_gradients({**mlp_terms, **terms})
    ins0, mlp_downs[0] = mlp_gradients(everyone[0], grad_all, weights[0])
    joined = [joined_rows(mlp_rows[1], which, 1, LAYERS, None) for which in range(2)]
    flat = after(flat, ins0, rec_flat[1], input_grad, *smalls[0], *joined, *mlp_downs)[0]
    pieces0 = rec_pieces(flat)
    rec_flat[0] = lax.all_gather(pieces0, "section", axis=0, tiled=False)
    mlp_rows[0] = to_rows(after(ins0, pieces0)[0])
    mlp_results = tuple(
        joined_rows(mlp_rows[0], which, 0, LAYERS, joined[which]) for which in range(2)
    ) + (jnp.stack(mlp_downs),)
    rec_flat[0] = after(rec_flat[0], *mlp_results)[0]
    results = []
    for layer in range(LAYERS):
        channels, norms = smalls[layer]
        results.append(
            rec_gradients(rec_flat[layer])
            + (
                channels[:CONV],
                channels[CONV],
                channels[CONV + 1],
                channels[CONV + 2],
                channels[CONV + 3],
                norms[0],
                norms[1],
            )
        )
    stacked = tuple(high(jnp.stack(parts)) for parts in zip(*results))
    return (output, input_grad) + stacked + mlp_results


def solution(mesh):
    return jax.shard_map(
        local,
        mesh=mesh,
        in_specs=(
            P(None, "dp", "section"),
            P(None, "dp", "section"),
            P(),
            P(None, "dp", None),
            P(None, "dp", None),
            P(None, "dp", None),
            P(None, None, "dp", None),
            P(None, None, "dp", None),
            P(None, None, "dp"),
            P(None, "dp"),
            P(None, "dp"),
            P(None, "dp"),
            P(None, "dp"),
            P(None, "dp"),
            P(None, "dp"),
            P(None, "dp", None),
            P(None, "dp", None),
            P(None, "dp", None),
        ),
        out_specs=(
            P(None, "dp", "section"),
            P(None, "dp", "section"),
            P(None, "dp", None),
            P(None, "dp", None),
            P(None, "dp", None),
            P(None, None, "dp", None),
            P(None, None, "dp", None),
            P(None, None, "dp"),
            P(None, "dp"),
            P(None, "dp"),
            P(None, "dp"),
            P(None, "dp"),
            P(None, "dp"),
            P(None, "dp"),
            P(None, "dp", None),
            P(None, "dp", None),
            P(None, "dp", None),
        ),
        check_vma=False,
    )
```

```python
import jax
import jax.numpy as jnp
from jax import lax
from jax.experimental import pallas as pl
from jax.experimental.pallas import tpu as pltpu
from jax.sharding import PartitionSpec as P

D = 2048
H = 10
BW = 256
F = 6144
R = 2560
CONV = 4
MICRO = 2
LAYERS = 2
MARGIN = CONV - 1
WIN = 2 * BW

EPS = 1e-06
LRU_EPS = 0.04
RATE_SCALE = 8.0


def low(value):
    return value.astype(jnp.bfloat16)


def high(value):
    return value.astype(jnp.float32)


def dot(left, right):
    return jnp.dot(left, right, preferred_element_type=jnp.float32)


def dot_nt(left, right):
    return lax.dot_general(
        left, right, (((1,), (1,)), ((), ())), preferred_element_type=jnp.float32
    )


def dot_tn(left, right):
    return lax.dot_general(
        left, right, (((0,), (0,)), ((), ())), preferred_element_type=jnp.float32
    )


def rms_scale(values, scales):
    return values * lax.rsqrt(jnp.mean(values * values, axis=-1, keepdims=True) + EPS) * scales


def meeting_order(count):
    return list(range(0, count, 2)) + list(range(1, count, 2))


def swapped(value, offset):
    count = lax.axis_size("dp")
    return lax.ppermute(value, "dp", [(at, at ^ offset) for at in range(count)])


def gather_rows(block):
    count = lax.axis_size("dp")
    same_core = jnp.concatenate([block] + [swapped(block, k) for k in range(2, count, 2)], axis=0)
    other_core = swapped(same_core, 1)
    return jnp.concatenate([same_core, other_core], axis=0)


def scatter_product(product, left):
    count = lax.axis_size("dp")
    half = left.shape[0] // 2
    rows = left.shape[0] // count
    away = swapped(low(product(left[half:])), 1)
    here = product(left[:half]) + high(away)
    total = here[:rows]
    for k in range(2, count, 2):
        piece = here[(k // 2) * rows : (k // 2 + 1) * rows]
        total = total + high(swapped(low(piece), k))
    return total


def spread(pack):
    return lax.all_to_all(pack, "dp", 0, 0, tiled=False)


def section_sum(chunks):
    return lax.psum_scatter(chunks, "section", scatter_dimension=0, tiled=False)


def all_rows(block):
    return lax.all_gather(block, ("dp", "section"), axis=0, tiled=True)


def other_planes(value):
    count = lax.axis_size("section")
    return [
        lax.ppermute(value, "section", [(at, at ^ k) for at in range(count)])
        for k in range(1, count)
    ]


def columns_apart(first, second, layer, count):
    rows, columns = first.shape[1], first.shape[2] // count
    if columns % 128:
        parts = [
            part[layer].reshape(rows, count, columns).transpose(1, 0, 2)
            for part in (first, second)
        ]
        return jnp.concatenate(parts, axis=2)

    def kernel(first_ref, second_ref, out_ref):
        out_ref[0, :, :columns] = first_ref[0]
        out_ref[0, :, columns:] = second_ref[0]

    return pl.pallas_call(
        kernel,
        out_shape=jax.ShapeDtypeStruct((count, rows, 2 * columns), first.dtype),
        grid=(count,),
        in_specs=[pl.BlockSpec((1, rows, columns), lambda at: (layer, 0, at))] * 2,
        out_specs=pl.BlockSpec((1, rows, 2 * columns), lambda at: (at, 0, 0)),
        cost_estimate=pl.CostEstimate(
            flops=0, transcendentals=0, bytes_accessed=8 * count * rows * columns
        ),
        compiler_params=pltpu.CompilerParams(vmem_limit_bytes=16 * 1024 * 1024),
    )(first, second)


def packed_columns(branch, gate, blocks, layer, filler):
    count, rows, extra = blocks.shape
    own = R // count
    width = WIN + own + filler + extra
    if own % 64:
        packs = []
        for device in range(count):
            begin, end, left, right = window_of(device, count)
            packs.append(
                jnp.concatenate(
                    own_first(branch[layer], device, count)
                    + [gate[layer][:, begin:end]]
                    + [jnp.zeros((rows, filler), branch.dtype), blocks[device]],
                    axis=1,
                )
            )
        return jnp.stack(packs)

    def kernel(branch_ref, gate_ref, blocks_ref, out_ref):
        for device in range(count):
            begin, end, left, right = window_of(device, count)
            at = 0
            for ref, start, stop in (
                (branch_ref, begin, end),
                (branch_ref, end, right),
                (branch_ref, left, begin),
                (gate_ref, begin, end),
            ):
                if stop > start:
                    out_ref[device, :, at : at + stop - start] = ref[0, :, start:stop]
                    at += stop - start
            if filler:
                out_ref[device, :, at : at + filler] = jnp.zeros((rows, filler), out_ref.dtype)
            out_ref[device, :, at + filler :] = blocks_ref[device]

    whole = pl.BlockSpec((1, rows, R), lambda at: (layer, 0, 0))
    return pl.pallas_call(
        kernel,
        out_shape=jax.ShapeDtypeStruct((count, rows, width), branch.dtype),
        grid=(1,),
        in_specs=[whole, whole, pl.BlockSpec((count, rows, extra), lambda at: (0, 0, 0))],
        out_specs=pl.BlockSpec((count, rows, width), lambda at: (0, 0, 0)),
        cost_estimate=pl.CostEstimate(
            flops=0, transcendentals=0, bytes_accessed=4 * count * rows * width
        ),
        compiler_params=pltpu.CompilerParams(vmem_limit_bytes=40 * 1024 * 1024),
    )(branch, gate, blocks)


def rows_kernel(part_ref, kept_ref, out_ref):
    del kept_ref
    out_ref[0] = part_ref[0].astype(jnp.float32)


def first_rows_kernel(part_ref, out_ref):
    out_ref[0] = part_ref[0].astype(jnp.float32)


def joined_rows(part, which, layer, layers, out):
    count, rows, columns = part.shape[0], part.shape[1], part.shape[2] // 2
    if columns % 128:
        part = part[:, :, which * columns : (which + 1) * columns]
        whole = jnp.zeros((layers, rows, count * columns), jnp.float32) if out is None else out
        piece = high(part.transpose(1, 0, 2).reshape(1, rows, -1))
        return lax.dynamic_update_slice_in_dim(whole, piece, layer, 0)
    operands = [part] + ([] if out is None else [out])
    return pl.pallas_call(
        first_rows_kernel if out is None else rows_kernel,
        out_shape=jax.ShapeDtypeStruct((layers, rows, count * columns), jnp.float32),
        grid=(count,),
        in_specs=[pl.BlockSpec((1, rows, columns), lambda at: (at, 0, which))]
        + [pl.BlockSpec(memory_space=pl.ANY)] * (len(operands) - 1),
        out_specs=pl.BlockSpec((1, rows, columns), lambda at: (layer, 0, at)),
        input_output_aliases={1: 0} if len(operands) > 1 else {},
        cost_estimate=pl.CostEstimate(
            flops=0, transcendentals=0, bytes_accessed=6 * count * rows * columns
        ),
        compiler_params=pltpu.CompilerParams(vmem_limit_bytes=16 * 1024 * 1024),
    )(*operands)


def after(value, *others):
    return lax.optimization_barrier((value,) + others)


def after_all(values, *others):
    return lax.optimization_barrier(tuple(values) + others)[: len(values)]


def lane_blocks(value, width):
    rows, columns = value.shape[-2:]
    split = value.reshape(value.shape[:-1] + (columns // width, width))
    return jnp.swapaxes(split, -3, -2).reshape(value.shape[:-2] + (-1, width))


def whole_rows(value, rows):
    blocks = value.shape[-2] // rows
    split = value.reshape(value.shape[:-2] + (blocks, rows, value.shape[-1]))
    return jnp.swapaxes(split, -3, -2).reshape(value.shape[:-2] + (rows, -1))


def window_of(device, count):
    own = R // count
    first_block = min(own * device // BW, H - 2)
    return own * device, own * (device + 1), BW * first_block, BW * first_block + WIN


def own_first(matrix, device, count):
    begin, end, left, right = window_of(device, count)
    return [matrix[:, begin:end], matrix[:, end:right], matrix[:, left:begin]]


def turned(value, axis, shift):
    size = value.shape[axis]
    twice = jnp.concatenate([value, value], axis=axis)
    return lax.dynamic_slice_in_dim(twice, jnp.mod(shift, size), size, axis)


def forward_scan_kernel(decay_ref, drive_ref, reach_ref, state_ref):
    rows = decay_ref.shape[1]
    reach = decay_ref[:, 0, :]
    state = drive_ref[:, 0, :]
    reach_ref[:, 0, :] = reach
    state_ref[:, 0, :] = state
    for row in range(1, rows):
        decay = decay_ref[:, row, :]
        state = decay * state + drive_ref[:, row, :]
        reach = decay * reach
        reach_ref[:, row, :] = reach
        state_ref[:, row, :] = state


def backward_scan_kernel(decay_ref, grad_ref, reach_ref, local_ref, top_ref):
    rows = decay_ref.shape[1]
    reach = jnp.ones_like(decay_ref[:, 0, :])
    local = grad_ref[:, rows - 1, :]
    reach_ref[:, rows - 1, :] = reach
    local_ref[:, rows - 1, :] = local
    for row in range(rows - 2, -1, -1):
        decay = decay_ref[:, row + 1, :]
        local = decay * local + grad_ref[:, row, :]
        reach = decay * reach
        reach_ref[:, row, :] = reach
        local_ref[:, row, :] = local
    top_ref[0] = decay_ref[:, 0, :] * reach
    top_ref[1] = decay_ref[:, 0, :] * local


def carry_kernel(reverse, where_ref, totals_ref, carry_ref):
    planes, count = totals_ref.shape[0], totals_ref.shape[2]
    me, rank = where_ref[0], where_ref[1]
    state = jnp.zeros(carry_ref.shape[1:], jnp.float32)
    for step in range(count):
        device = count - 1 - step if reverse else step
        offset = jnp.bitwise_xor(me, device)
        at = offset // 2 + (offset % 2) * (count // 2)
        for plane in range(planes - 1, -1, -1) if reverse else range(planes):

            @pl.when(rank == plane)
            def _(state=state, at=at):
                carry_ref[at] = state

            met = jnp.bitwise_xor(rank, plane)
            state = totals_ref[met, 0, at] * state + totals_ref[met, 1, at]


VMEM_SPEC = pl.BlockSpec(memory_space=pltpu.VMEM)


def in_vmem(kernel, shapes, *operands, scalars=0):
    specs = [pl.BlockSpec(memory_space=pltpu.SMEM)] * scalars
    return pl.pallas_call(
        kernel,
        out_shape=tuple(jax.ShapeDtypeStruct(shape, jnp.float32) for shape in shapes),
        in_specs=specs + [VMEM_SPEC] * (len(operands) - scalars),
        out_specs=tuple(VMEM_SPEC for _ in shapes),
        compiler_params=pltpu.CompilerParams(vmem_limit_bytes=40 * 1024 * 1024),
    )(*operands)


def carried(totals, reverse):
    count = lax.axis_size("dp")
    channels = totals.shape[-1]
    totals = totals.reshape(2, count, MICRO, channels)
    everything = jnp.stack([totals] + other_planes(totals))
    where = jnp.stack([lax.axis_index("dp"), lax.axis_index("section")]).astype(jnp.int32)

    def kernel(where_ref, totals_ref, carry_ref):
        carry_kernel(reverse, where_ref, totals_ref, carry_ref)

    (carry,) = in_vmem(kernel, [(count, MICRO, channels)], where, everything, scalars=1)
    return carry.reshape(count * MICRO, channels)


def gelu_product(states, side):
    return states * jax.nn.gelu(side)


def gated_gelu(gate_val, up_val):
    return jax.nn.gelu(gate_val) * up_val


def local(
    inputs,
    cotangent,
    resets,
    branch_in,
    gate_in,
    rec_out,
    rate_gate,
    input_gate,
    conv_taps,
    conv_bias,
    rate_bias,
    input_bias,
    decay_param,
    norm_rec,
    norm_mlp,
    mlp_gate,
    mlp_up,
    mlp_down,
):
    planes = lax.axis_size("section")
    count = lax.axis_size("dp")
    rank = lax.axis_index("section")
    me = lax.axis_index("dp")
    block_rows = inputs.shape[1]
    length = block_rows // planes
    seq = resets.shape[1]
    rows = MICRO * length
    segments = MICRO * count
    tokens = segments * length
    own = R // count
    wide = F // count
    strip = D // count
    thin = strip // planes
    filler = D // 2 - BW // 2 - WIN - own
    order = jnp.array(meeting_order(count), jnp.int32)
    devices = jnp.bitwise_xor(me, order)

    small = jnp.concatenate(
        [
            norm_rec,
            norm_mlp,
            conv_taps.reshape(LAYERS, CONV * own),
            conv_bias,
        ],
        axis=1,
    )
    small_all = lax.all_gather(small, "dp", axis=0, tiled=False)
    own_begin = own * me
    first_block = jnp.minimum(own_begin // BW, H - 2)
    shift = own_begin - BW * first_block

    def small_whole(layer, begin, each):
        return small_all[:, layer, begin : begin + each].reshape(count * each)

    def packed_in(layer, shared):
        def cut(value, axis):
            if not shared:
                return value
            size = value.shape[axis] // planes
            return lax.dynamic_slice_in_dim(value, size * later_rank, size, axis)

        gates = cut(jnp.stack([rate_gate[layer], input_gate[layer]]), 2)
        blocks = []
        for device in range(count):
            begin, end, left, right = window_of(device, count)
            height = thin if shared else strip
            blocks.append(gates[:, left // BW : right // BW].reshape(height, -1))
        branch, gate, at = branch_in, gate_in, layer
        if shared:
            branch, gate, at = cut(branch_in[layer:], 1), cut(gate_in[layer:], 1), 0
        return packed_columns(branch, gate, jnp.stack(blocks), at, filler)

    def by_features(value):
        moved = value.reshape(MICRO, length, D)
        return lax.all_to_all(moved, "section", split_axis=2, concat_axis=1, tiled=True)

    both_ends = lax.all_to_all(
        jnp.concatenate([inputs, cotangent], axis=0), "section", 1, 2, tiled=True
    )
    stream, grad = both_ends[:MICRO].reshape(rows, D), both_ends[MICRO:].reshape(rows, D)
    top_grad_all = all_rows(grad)
    in_moved = [None] * LAYERS
    mlp_moved = [None] * LAYERS
    first_pack = packed_in(0, False)
    later_rank = after(rank, first_pack)[0]
    in_moved[0] = spread(after(first_pack, small_all, stream)[0])
    normed = low(rms_scale(high(stream), high(small_whole(0, 0, strip))))
    first_normed = gather_rows(normed)
    in_width = WIN + own + filler
    first_both = dot(first_normed, in_moved[0].reshape(D, -1)[:, :in_width])
    in_share = spread(after(packed_in(1, True), first_both)[0])
    in_moved[1] = lax.all_gather(in_share, "section", axis=1, tiled=True)
    mlp_moved[0] = spread(after(columns_apart(mlp_gate, mlp_up, 0, count), in_share)[0])
    def layer_weights(layer):
        in_weight = in_moved[layer].reshape(D, -1)
        blocks = in_weight[:, WIN + own + filler :]
        parts = planes if layer else 1
        blocks = blocks.reshape(count, parts, 2, 2, BW // count // parts, BW)
        blocks = blocks.transpose(2, 3, 0, 1, 4, 5).reshape(2, 2, BW, BW)
        in_weight = in_weight[:, : WIN + own + filler]
        empty = jnp.zeros((BW, BW), jnp.bfloat16)
        gate_weights = []
        for which in range(2):
            whole = jnp.concatenate(
                [
                    jnp.concatenate([blocks[which, 0], empty], axis=1),
                    jnp.concatenate([empty, blocks[which, 1]], axis=1),
                ],
                axis=0,
            )
            gate_weights.append(turned(turned(whole, 0, shift), 1, shift)[:, :own])
        taps = jnp.concatenate(
            [
                small_all[:, layer, 2 * strip :].reshape(count, CONV + 1, own),
            ],
            axis=0,
        )
        taps = taps.transpose(1, 0, 2).reshape(CONV + 1, R)
        taps = lax.dynamic_slice_in_dim(taps, BW * first_block, WIN, 1)
        taps = high(turned(taps, 1, shift))
        return (
            {
                "in": in_weight,
                "gates": jnp.concatenate(gate_weights, axis=1),
                "out": rec_out[layer],
                "taps": taps[:CONV],
                "bias": taps[CONV],
                "rate_bias": high(rate_bias[layer]),
                "input_bias": high(input_bias[layer]),
                "decay": high(decay_param[layer]),
                "norm_rec": high(small_whole(layer, 0, strip)),
                "norm_mlp": high(small_whole(layer, strip, strip)),
                "down": mlp_down[layer],
            }
        )

    keep = (1 - resets).astype(jnp.float32)
    padded = jnp.concatenate(
        [
            jnp.ones((MICRO, MARGIN), jnp.float32),
            keep,
            jnp.zeros((MICRO, length), jnp.float32),
        ],
        axis=1,
    )
    reach = 2 * MARGIN
    window = jnp.concatenate(
        [
            padded[:, :seq].reshape(MICRO, count, planes, length),
            padded[:, length : length + seq].reshape(MICRO, count, planes, length)[..., :reach],
        ],
        axis=3,
    )
    window = lax.dynamic_index_in_dim(window, rank, 2, keepdims=False)
    same = (devices[:, None] == jnp.arange(count)[None, :]).astype(jnp.float32)
    window = jnp.einsum("pj,mjr->pmr", same, window, precision=lax.Precision.HIGHEST)
    window = window.reshape(segments, length + reach)
    usable = [jnp.ones((segments, length + MARGIN, 1), jnp.float32)]
    for lag in range(1, CONV):
        begin = MARGIN - lag + 1
        usable.append(usable[-1] * window[:, begin : begin + length + MARGIN, None])
    carry_mask = window[:, MARGIN : MARGIN + length, None]

    edge_from = {}
    for step, plane in ((1, 0), (-1, planes - 1)):
        wanted = devices - jnp.where(rank == plane, step, 0)
        edge_from[step] = (wanted[:, None] == devices[None, :]).astype(jnp.float32)

    def edge(rows_out, step):
        came = lax.ppermute(
            rows_out, "section", [(at, (at + step) % planes) for at in range(planes)]
        )
        flat = came.reshape(count, -1)
        chosen = edge_from[step]
        moved = sum(chosen[:, q : q + 1] * flat[q][None] for q in range(count))
        return moved.reshape(rows_out.shape)

    def lru_parts(weight):
        rate = RATE_SCALE * jax.nn.softplus(-weight["decay"])
        return rate

    def rec_forward(section_in, weight, normed, both, late):
        if normed is None:
            normed = gather_rows(low(rms_scale(high(section_in), weight["norm_rec"])))
            both = dot(normed, weight["in"])
        branch = both[:, :WIN].reshape(segments, length, WIN)
        side = both[:, WIN : WIN + own].reshape(segments, length, own)
        extended = jnp.concatenate([edge(branch[:, length - MARGIN :], 1), branch], axis=1)
        conved = weight["bias"] + weight["taps"][0] * branch
        for lag in range(1, CONV):
            conved = (
                conved
                + weight["taps"][lag]
                * usable[lag][:, :length]
                * extended[:, MARGIN - lag : MARGIN - lag + length]
            )
        conv_low = low(conved).reshape(tokens, WIN)
        raw = dot(conv_low, weight["gates"])
        rate_sig = jax.nn.sigmoid(raw[:, :own] + weight["rate_bias"])
        input_sig = jax.nn.sigmoid(raw[:, own:] + weight["input_bias"])
        rate_sig = rate_sig.reshape(segments, length, own)
        input_sig = input_sig.reshape(segments, length, own)
        conved = conved[:, :, :own]
        decays = jnp.exp(-lru_parts(weight) * rate_sig) * carry_mask
        root = jnp.sqrt(1.0 + LRU_EPS - decays * decays)
        drives = root * input_sig * conved
        shape = (segments, length, own)
        cumulative, partial = in_vmem(forward_scan_kernel, [shape, shape], decays, drives)
        carry = carried(jnp.stack([cumulative[:, -1], partial[:, -1]]), False)
        states = partial + cumulative * carry[:, None]
        mixture = low(gelu_product(states, side)).reshape(tokens, own)
        mixture = after(mixture, *late)[0]
        result = high(section_in) + scatter_product(
            lambda left: dot(left, weight["out"]), mixture
        )
        kept = {
            "section_in": section_in,
            "normed": normed,
            "extended": extended,
            "side": side,
            "conved": conved,
            "conv_low": conv_low,
            "rate_sig": rate_sig,
            "input_sig": input_sig,
            "decays": decays,
            "root": root,
            "carry": carry,
            "states": states,
            "mixture": mixture,
        }
        return low(result), kept

    def mlp_forward(section_in, weight, late):
        normed = low(rms_scale(high(section_in), weight["norm_mlp"]))
        here = normed
        normed = gather_rows(normed)
        both = dot(normed, weight["mlp"])
        gate_val, up_val = both[:, :wide], both[:, wide:]
        hidden = after(low(gated_gelu(gate_val, up_val)), *late)[0]
        result = high(section_in) + scatter_product(
            lambda left: dot(left, weight["down"]), hidden
        )
        kept = {
            "section_in": section_in,
            "normed": here,
            "hidden": hidden,
            "gate_val": gate_val,
            "up_val": up_val,
        }
        return low(result), kept

    def mlp_backward(grad, weight, kept):
        grad_all = gather_rows(grad)
        grad_hidden = dot_nt(grad_all, weight["down"])
        _, pull = jax.vjp(gated_gelu, kept["gate_val"], kept["up_val"])
        gate_grad, up_grad = pull(grad_hidden)
        both = jnp.concatenate([low(gate_grad), low(up_grad)], axis=1)
        grad_normed = scatter_product(lambda left: dot_nt(left, weight["mlp"]), both)
        _, pull = jax.vjp(rms_scale, high(kept["section_in"]), weight["norm_mlp"])
        grad_in, norm_grad = pull(grad_normed)
        return low(grad_in + high(grad)), {"norm_mlp": norm_grad}

    def rec_backward(grad, weight, kept, early):
        grad_all = gather_rows(grad)
        shape = (segments, length, own)
        grad_mixture = dot_nt(grad_all, weight["out"]).reshape(shape)
        _, pull = jax.vjp(gelu_product, kept["states"], kept["side"])
        grad_states0, grad_side = pull(grad_mixture)
        decays, root = kept["decays"], kept["root"]
        reached, partial, top = in_vmem(
            backward_scan_kernel,
            [shape, shape, (2, segments, own)],
            decays,
            grad_states0,
        )
        carry = carried(after(top, *early)[0], True)
        grad_states = partial + reached * carry[:, None]
        previous = jnp.concatenate([kept["carry"][:, None], kept["states"][:, :-1]], axis=1)
        conved, rate_sig, input_sig = kept["conved"], kept["rate_sig"], kept["input_sig"]
        grad_decays = grad_states * (previous - input_sig * conved * decays / root)
        slope = grad_decays * decays * rate_sig
        rate_grad = slope * (-lru_parts(weight)) * (1.0 - rate_sig)
        input_grad = grad_states * root * conved * input_sig * (1.0 - input_sig)
        raw_grad = low(
            jnp.concatenate([rate_grad, input_grad], axis=2).reshape(tokens, 2 * own)
        )
        spare = jnp.zeros((segments, length, WIN - own), jnp.float32)
        conv_grad = jnp.concatenate([grad_states * root * input_sig, spare], axis=2)
        conv_grad = conv_grad + dot_nt(raw_grad, weight["gates"]).reshape(segments, length, WIN)
        longer = jnp.concatenate([conv_grad, edge(conv_grad[:, :MARGIN], -1)], axis=1)
        branch_grad = weight["taps"][0] * conv_grad
        taps_grad = [jnp.sum(kept["extended"][:, MARGIN:] * conv_grad, axis=(0, 1))]
        for lag in range(1, CONV):
            branch_grad = (
                branch_grad
                + weight["taps"][lag]
                * usable[lag][:, lag : lag + length]
                * longer[:, lag : lag + length]
            )
            taps_grad.append(
                jnp.sum(
                    usable[lag][:, :length]
                    * kept["extended"][:, MARGIN - lag : MARGIN - lag + length]
                    * conv_grad,
                    axis=(0, 1),
                )
            )
        both = low(
            jnp.concatenate(
                [branch_grad, grad_side, jnp.zeros((segments, length, filler), jnp.float32)],
                axis=2,
            ).reshape(tokens, WIN + own + filler)
        )
        grad_normed = scatter_product(lambda left: dot_nt(left, weight["in"]), both)
        _, pull = jax.vjp(rms_scale, high(kept["section_in"]), weight["norm_rec"])
        grad_in, norm_grad = pull(grad_normed)
        terms = {
            "in": dot_tn(kept["normed"], both),
            "out": dot_tn(kept["mixture"], grad_all),
            "gates": dot_tn(kept["conv_low"], raw_grad),
            "taps": jnp.stack(taps_grad + [jnp.sum(conv_grad, axis=(0, 1))]),
            "rate_bias": jnp.sum(rate_grad, axis=(0, 1)),
            "input_bias": jnp.sum(input_grad, axis=(0, 1)),
            "decay": jnp.sum(slope, axis=(0, 1)) * RATE_SCALE * jax.nn.sigmoid(-weight["decay"]),
            "norm_rec": norm_grad,
            "in_grads": both,
        }
        return low(grad_in + high(grad)), terms

    def mlp_gradients(normed, grad_all, weight):
        both = dot(normed, weight["mlp"])
        product, pull = jax.vjp(gated_gelu, both[:, :wide], both[:, wide:])
        gate_grad, up_grad = pull(dot_nt(grad_all, weight["down"]))
        both_grad = jnp.concatenate([low(gate_grad), low(up_grad)], axis=1)
        return low(dot_tn(normed, both_grad)), dot_tn(low(product), grad_all)

    def to_rows(part):
        return spread(part.reshape(count, strip, 2 * wide))

    def rec_shares(terms):
        each = BW // count // planes
        blocks = []
        for which in range(2):
            square = jnp.concatenate(
                [
                    terms["gates"][:, which * own : (which + 1) * own],
                    jnp.zeros((WIN, WIN - own), jnp.float32),
                ],
                axis=1,
            )
            square = turned(turned(square, 0, -shift), 1, -shift)
            blocks.append(jnp.stack([square[:BW, :BW], square[BW:, BW:]]))
        blocks = low(jnp.stack(blocks)).reshape(2, 2, count, planes, each, 2, BW // 2)
        blocks = blocks.transpose(3, 2, 0, 1, 4, 5, 6).reshape(planes, count, 8 * each, BW // 2)
        blocks = blocks.reshape(planes, count, thin, -1)
        mixed = low(terms["in"]).reshape(count, planes, thin, WIN + own + filler)
        mixed = jnp.concatenate([mixed.transpose(1, 0, 2, 3), blocks], axis=3)
        width = mixed.shape[-1]
        out = low(terms["out"]).reshape(planes, own // planes, D)
        flat = jnp.concatenate(
            [mixed.reshape(planes, count * thin, width), lane_blocks(out, width)], axis=1
        )
        return flat

    def rec_pieces(flat):
        each = BW // count // planes
        width = WIN + own + filler + 8 * each * (BW // 2) // thin
        out = whole_rows(flat[count * thin :], own // planes)
        mine = spread(flat[: count * thin].reshape(count, thin, width))
        blocks = mine[:, :, WIN + own + filler :].reshape(count, 2, 2, each, BW)
        mine = high(mine)
        gate = low(mine[:, :, WIN : WIN + own]).transpose(1, 0, 2).reshape(thin, R)
        branch = mine[:, :, :own].transpose(1, 0, 2).reshape(thin, R)
        for device in range(count):
            begin, end, left, right = window_of(device, count)
            if right > end:
                piece = mine[device, :, own : own + right - end]
                branch = branch + jnp.pad(piece, ((0, 0), (end, R - right)))
            if begin > left:
                piece = mine[device, :, own + right - end : WIN]
                branch = branch + jnp.pad(piece, ((0, 0), (left, R - begin)))
        totals = [0.0] * H
        for device in range(count):
            first = window_of(device, count)[2] // BW
            for at in range(2):
                totals[first + at] = totals[first + at] + high(blocks[device, :, at])
        gates = low(jnp.stack(totals, axis=1))
        return jnp.concatenate(
            [
                lane_blocks(low(branch), WIN),
                lane_blocks(gate, WIN),
                lane_blocks(out, WIN),
                lane_blocks(gates.reshape(-1, 2 * BW), WIN),
            ],
            axis=0,
        )

    def rec_gradients(flat):
        each = BW // count // planes
        sizes = [thin * R // WIN, thin * R // WIN, own // planes * D // WIN]
        at = [0, sizes[0], sizes[0] + sizes[1], sum(sizes)]
        branch = whole_rows(flat[:, at[0] : at[1]], thin).reshape(strip, R)
        gate = whole_rows(flat[:, at[1] : at[2]], thin).reshape(strip, R)
        out = whole_rows(flat[:, at[2] : at[3]], own // planes).reshape(own, D)
        gates = flat[:, at[3] :].reshape(planes, 2, H, each, BW)
        gates = gates.transpose(1, 2, 0, 3, 4).reshape(2, H, BW // count, BW)
        return branch, gate, out, gates[0], gates[1]

    def small_gradients(terms):
        taps = turned(terms["taps"], 1, -shift)
        taps = lax.dynamic_update_slice(
            jnp.zeros((CONV + 1, R), jnp.float32), taps, (0, BW * first_block)
        )
        owned = jnp.stack([terms["rate_bias"], terms["input_bias"], terms["decay"]])
        owned = lax.dynamic_update_slice(
            jnp.zeros((3, R), jnp.float32), owned, (0, own_begin)
        )
        channels = jnp.concatenate([taps, owned], axis=0)
        norms = jnp.stack([terms["norm_rec"], terms["norm_mlp"]])
        pack = jnp.concatenate(
            [
                channels.reshape(CONV + 4, count, own).transpose(1, 0, 2).reshape(count, -1),
                norms.reshape(2, count, strip).transpose(1, 0, 2).reshape(count, -1),
            ],
            axis=1,
        )
        mine = jnp.sum(spread(pack), axis=0)
        mine = mine.reshape(-1, 128)
        mine = (mine + sum(other_planes(mine))).reshape(-1)
        channels = mine[: (CONV + 4) * own].reshape(CONV + 4, own)
        norms = mine[(CONV + 4) * own :].reshape(2, strip)
        return channels, norms

    weights = [layer_weights(0)]
    weights[0]["mlp"] = mlp_moved[0].reshape(D, 2 * wide)
    kept = []
    everyone = [None] * LAYERS
    top = LAYERS - 1
    for layer in range(LAYERS):
        weight = weights[layer]
        first = layer == 0
        stream, kept_rec = rec_forward(
            stream,
            weight,
            first_normed if first else None,
            first_both if first else None,
            [top_grad_all] if first else [],
        )
        if first:
            shares = [
                lax.dynamic_slice_in_dim(part[1:], thin * rank, thin, 1)
                for part in (mlp_gate, mlp_up)
            ]
            share = spread(after(columns_apart(*shares, 0, count), mlp_moved[0])[0])
            share = after(share, in_moved[1])[0]
            mlp_moved[1] = lax.all_gather(share, "section", axis=1, tiled=True)
            weights.append(layer_weights(1))
        else:
            everyone[0] = all_rows(after(kept[0][1]["normed"], kept_rec["mixture"])[0])
        stream, kept_mlp = mlp_forward(stream, weight, [share] if first else [])
        if first:
            weights[1]["mlp"] = mlp_moved[1].reshape(D, 2 * wide)
        else:
            everyone[1] = all_rows(after(kept_mlp["normed"], stream)[0])
        kept.append((kept_rec, kept_mlp))
    output = by_features(stream)
    mlp_downs = [None] * LAYERS
    mlp_rows = [None] * LAYERS
    rec_flat = [None] * LAYERS
    smalls = [None] * LAYERS

    grad_in = grad
    grad, mlp_terms = mlp_backward(grad_in, weights[1], kept[1][1])
    ins1, mlp_downs[1] = mlp_gradients(everyone[1], top_grad_all, weights[1])
    grad, everyone[0] = after(grad, everyone[0])
    grad, terms = rec_backward(grad, weights[1], kept[1][0], [output])
    grad, everyone[1] = after(grad, everyone[1])
    flat = section_sum(rec_shares(terms))
    smalls[1] = small_gradients({**mlp_terms, **terms})
    mlp_rows[1] = to_rows(ins1)

    grad_in = grad
    grad_mid, mlp_terms = mlp_backward(grad_in, weights[0], kept[0][1])
    pieces1 = rec_pieces(after(flat, grad_mid)[0])
    grad_all = all_rows(grad_in)
    grad, terms = rec_backward(grad_mid, weights[0], kept[0][0], [pieces1])
    input_grad = by_features(grad)
    flat = rec_shares(terms)
    grad_all = after(grad_all, flat)[0]
    flat = section_sum(flat)
    rec_flat[1] = lax.all_gather(after(pieces1, flat)[0], "section", axis=0, tiled=False)
    smalls[0] = small_gradients({**mlp_terms, **terms})
    ins0, mlp_downs[0] = mlp_gradients(everyone[0], grad_all, weights[0])
    joined = [joined_rows(mlp_rows[1], which, 1, LAYERS, None) for which in range(2)]
    flat = after(flat, ins0, mlp_rows[1])[0]
    pieces0 = rec_pieces(flat)
    rec_flat[0] = lax.all_gather(pieces0, "section", axis=0, tiled=False)
    mlp_rows[0] = to_rows(after(ins0, pieces0)[0])
    mlp_results = tuple(
        joined_rows(mlp_rows[0], which, 0, LAYERS, joined[which]) for which in range(2)
    ) + (jnp.stack(mlp_downs),)
    rec_flat[0] = after(rec_flat[0], *mlp_results, input_grad, *smalls[0])[0]
    results = []
    for layer in range(LAYERS):
        channels, norms = smalls[layer]
        results.append(
            rec_gradients(rec_flat[layer])
            + (
                channels[:CONV],
                channels[CONV],
                channels[CONV + 1],
                channels[CONV + 2],
                channels[CONV + 3],
                norms[0],
                norms[1],
            )
        )
    stacked = tuple(high(jnp.stack(parts)) for parts in zip(*results))
    return (output, input_grad) + stacked + mlp_results


def solution(mesh):
    return jax.shard_map(
        local,
        mesh=mesh,
        in_specs=(
            P(None, "dp", "section"),
            P(None, "dp", "section"),
            P(),
            P(None, "dp", None),
            P(None, "dp", None),
            P(None, "dp", None),
            P(None, None, "dp", None),
            P(None, None, "dp", None),
            P(None, None, "dp"),
            P(None, "dp"),
            P(None, "dp"),
            P(None, "dp"),
            P(None, "dp"),
            P(None, "dp"),
            P(None, "dp"),
            P(None, "dp", None),
            P(None, "dp", None),
            P(None, "dp", None),
        ),
        out_specs=(
            P(None, "dp", "section"),
            P(None, "dp", "section"),
            P(None, "dp", None),
            P(None, "dp", None),
            P(None, "dp", None),
            P(None, None, "dp", None),
            P(None, None, "dp", None),
            P(None, None, "dp"),
            P(None, "dp"),
            P(None, "dp"),
            P(None, "dp"),
            P(None, "dp"),
            P(None, "dp"),
            P(None, "dp"),
            P(None, "dp", None),
            P(None, "dp", None),
            P(None, "dp", None),
        ),
        check_vma=False,
    )
```

```python
import jax
import jax.numpy as jnp
from jax import lax
from jax.experimental import pallas as pl
from jax.experimental.pallas import tpu as pltpu
from jax.sharding import PartitionSpec as P

D = 2048
H = 10
BW = 256
F = 6144
R = 2560
CONV = 4
MICRO = 2
LAYERS = 2
MARGIN = CONV - 1
WIN = 2 * BW

EPS = 1e-06
LRU_EPS = 0.04
RATE_SCALE = 8.0


def low(value):
    return value.astype(jnp.bfloat16)


def high(value):
    return value.astype(jnp.float32)


def dot(left, right):
    return jnp.dot(left, right, preferred_element_type=jnp.float32)


def dot_nt(left, right):
    return lax.dot_general(
        left, right, (((1,), (1,)), ((), ())), preferred_element_type=jnp.float32
    )


def dot_tn(left, right):
    return lax.dot_general(
        left, right, (((0,), (0,)), ((), ())), preferred_element_type=jnp.float32
    )


def rms_scale(values, scales):
    return values * lax.rsqrt(jnp.mean(values * values, axis=-1, keepdims=True) + EPS) * scales


def meeting_order(count):
    return list(range(0, count, 2)) + list(range(1, count, 2))


def swapped(value, offset):
    count = lax.axis_size("dp")
    return lax.ppermute(value, "dp", [(at, at ^ offset) for at in range(count)])


def gather_rows(block):
    count = lax.axis_size("dp")
    same_core = jnp.concatenate([block] + [swapped(block, k) for k in range(2, count, 2)], axis=0)
    other_core = swapped(same_core, 1)
    return jnp.concatenate([same_core, other_core], axis=0)


def scatter_product(product, left):
    count = lax.axis_size("dp")
    half = left.shape[0] // 2
    rows = left.shape[0] // count
    away = swapped(low(product(left[half:])), 1)
    here = product(left[:half]) + high(away)
    total = here[:rows]
    for k in range(2, count, 2):
        piece = here[(k // 2) * rows : (k // 2 + 1) * rows]
        total = total + high(swapped(low(piece), k))
    return total


def spread(pack):
    return lax.all_to_all(pack, "dp", 0, 0, tiled=False)


def section_sum(chunks):
    return lax.psum_scatter(chunks, "section", scatter_dimension=0, tiled=False)


def all_rows(block):
    return lax.all_gather(block, ("dp", "section"), axis=0, tiled=True)


def other_planes(value):
    count = lax.axis_size("section")
    return [
        lax.ppermute(value, "section", [(at, at ^ k) for at in range(count)])
        for k in range(1, count)
    ]


def columns_apart(first, second, layer, count):
    rows, columns = first.shape[1], first.shape[2] // count
    if columns % 128:
        parts = [
            part[layer].reshape(rows, count, columns).transpose(1, 0, 2)
            for part in (first, second)
        ]
        return jnp.concatenate(parts, axis=2)

    def kernel(first_ref, second_ref, out_ref):
        out_ref[0, :, :columns] = first_ref[0]
        out_ref[0, :, columns:] = second_ref[0]

    return pl.pallas_call(
        kernel,
        out_shape=jax.ShapeDtypeStruct((count, rows, 2 * columns), first.dtype),
        grid=(count,),
        in_specs=[pl.BlockSpec((1, rows, columns), lambda at: (layer, 0, at))] * 2,
        out_specs=pl.BlockSpec((1, rows, 2 * columns), lambda at: (at, 0, 0)),
        cost_estimate=pl.CostEstimate(
            flops=0, transcendentals=0, bytes_accessed=8 * count * rows * columns
        ),
        compiler_params=pltpu.CompilerParams(vmem_limit_bytes=16 * 1024 * 1024),
    )(first, second)


def packed_columns(branch, gate, blocks, layer, filler):
    count, rows, extra = blocks.shape
    own = R // count
    width = WIN + own + filler + extra
    if own % 64:
        packs = []
        for device in range(count):
            begin, end, left, right = window_of(device, count)
            packs.append(
                jnp.concatenate(
                    own_first(branch[layer], device, count)
                    + [gate[layer][:, begin:end]]
                    + [jnp.zeros((rows, filler), branch.dtype), blocks[device]],
                    axis=1,
                )
            )
        return jnp.stack(packs)

    def kernel(branch_ref, gate_ref, blocks_ref, out_ref):
        for device in range(count):
            begin, end, left, right = window_of(device, count)
            at = 0
            for ref, start, stop in (
                (branch_ref, begin, end),
                (branch_ref, end, right),
                (branch_ref, left, begin),
                (gate_ref, begin, end),
            ):
                if stop > start:
                    out_ref[device, :, at : at + stop - start] = ref[0, :, start:stop]
                    at += stop - start
            if filler:
                out_ref[device, :, at : at + filler] = jnp.zeros((rows, filler), out_ref.dtype)
            out_ref[device, :, at + filler :] = blocks_ref[device]

    whole = pl.BlockSpec((1, rows, R), lambda at: (layer, 0, 0))
    return pl.pallas_call(
        kernel,
        out_shape=jax.ShapeDtypeStruct((count, rows, width), branch.dtype),
        grid=(1,),
        in_specs=[whole, whole, pl.BlockSpec((count, rows, extra), lambda at: (0, 0, 0))],
        out_specs=pl.BlockSpec((count, rows, width), lambda at: (0, 0, 0)),
        cost_estimate=pl.CostEstimate(
            flops=0, transcendentals=0, bytes_accessed=4 * count * rows * width
        ),
        compiler_params=pltpu.CompilerParams(vmem_limit_bytes=40 * 1024 * 1024),
    )(branch, gate, blocks)


def rows_kernel(part_ref, kept_ref, out_ref):
    del kept_ref
    out_ref[0] = part_ref[0].astype(jnp.float32)


def first_rows_kernel(part_ref, out_ref):
    out_ref[0] = part_ref[0].astype(jnp.float32)


def joined_rows(part, which, layer, layers, out):
    count, rows, columns = part.shape[0], part.shape[1], part.shape[2] // 2
    if columns % 128:
        part = part[:, :, which * columns : (which + 1) * columns]
        whole = jnp.zeros((layers, rows, count * columns), jnp.float32) if out is None else out
        piece = high(part.transpose(1, 0, 2).reshape(1, rows, -1))
        return lax.dynamic_update_slice_in_dim(whole, piece, layer, 0)
    operands = [part] + ([] if out is None else [out])
    return pl.pallas_call(
        first_rows_kernel if out is None else rows_kernel,
        out_shape=jax.ShapeDtypeStruct((layers, rows, count * columns), jnp.float32),
        grid=(count,),
        in_specs=[pl.BlockSpec((1, rows, columns), lambda at: (at, 0, which))]
        + [pl.BlockSpec(memory_space=pl.ANY)] * (len(operands) - 1),
        out_specs=pl.BlockSpec((1, rows, columns), lambda at: (layer, 0, at)),
        input_output_aliases={1: 0} if len(operands) > 1 else {},
        cost_estimate=pl.CostEstimate(
            flops=0, transcendentals=0, bytes_accessed=6 * count * rows * columns
        ),
        compiler_params=pltpu.CompilerParams(vmem_limit_bytes=16 * 1024 * 1024),
    )(*operands)


def after(value, *others):
    return lax.optimization_barrier((value,) + others)


def after_all(values, *others):
    return lax.optimization_barrier(tuple(values) + others)[: len(values)]


def lane_blocks(value, width):
    rows, columns = value.shape[-2:]
    split = value.reshape(value.shape[:-1] + (columns // width, width))
    return jnp.swapaxes(split, -3, -2).reshape(value.shape[:-2] + (-1, width))


def whole_rows(value, rows):
    blocks = value.shape[-2] // rows
    split = value.reshape(value.shape[:-2] + (blocks, rows, value.shape[-1]))
    return jnp.swapaxes(split, -3, -2).reshape(value.shape[:-2] + (rows, -1))


def window_of(device, count):
    own = R // count
    first_block = min(own * device // BW, H - 2)
    return own * device, own * (device + 1), BW * first_block, BW * first_block + WIN


def own_first(matrix, device, count):
    begin, end, left, right = window_of(device, count)
    return [matrix[:, begin:end], matrix[:, end:right], matrix[:, left:begin]]


def turned(value, axis, shift):
    size = value.shape[axis]
    twice = jnp.concatenate([value, value], axis=axis)
    return lax.dynamic_slice_in_dim(twice, jnp.mod(shift, size), size, axis)


def forward_scan_kernel(decay_ref, drive_ref, reach_ref, state_ref):
    rows = decay_ref.shape[1]
    reach = decay_ref[:, 0, :]
    state = drive_ref[:, 0, :]
    reach_ref[:, 0, :] = reach
    state_ref[:, 0, :] = state
    for row in range(1, rows):
        decay = decay_ref[:, row, :]
        state = decay * state + drive_ref[:, row, :]
        reach = decay * reach
        reach_ref[:, row, :] = reach
        state_ref[:, row, :] = state


def backward_scan_kernel(decay_ref, grad_ref, reach_ref, local_ref, top_ref):
    rows = decay_ref.shape[1]
    reach = jnp.ones_like(decay_ref[:, 0, :])
    local = grad_ref[:, rows - 1, :]
    reach_ref[:, rows - 1, :] = reach
    local_ref[:, rows - 1, :] = local
    for row in range(rows - 2, -1, -1):
        decay = decay_ref[:, row + 1, :]
        local = decay * local + grad_ref[:, row, :]
        reach = decay * reach
        reach_ref[:, row, :] = reach
        local_ref[:, row, :] = local
    top_ref[0] = decay_ref[:, 0, :] * reach
    top_ref[1] = decay_ref[:, 0, :] * local


def carry_kernel(reverse, where_ref, totals_ref, carry_ref):
    planes, count = totals_ref.shape[0], totals_ref.shape[2]
    me, rank = where_ref[0], where_ref[1]
    state = jnp.zeros(carry_ref.shape[1:], jnp.float32)
    for step in range(count):
        device = count - 1 - step if reverse else step
        offset = jnp.bitwise_xor(me, device)
        at = offset // 2 + (offset % 2) * (count // 2)
        for plane in range(planes - 1, -1, -1) if reverse else range(planes):

            @pl.when(rank == plane)
            def _(state=state, at=at):
                carry_ref[at] = state

            met = jnp.bitwise_xor(rank, plane)
            state = totals_ref[met, 0, at] * state + totals_ref[met, 1, at]


VMEM_SPEC = pl.BlockSpec(memory_space=pltpu.VMEM)


def in_vmem(kernel, shapes, *operands, scalars=0):
    specs = [pl.BlockSpec(memory_space=pltpu.SMEM)] * scalars
    return pl.pallas_call(
        kernel,
        out_shape=tuple(jax.ShapeDtypeStruct(shape, jnp.float32) for shape in shapes),
        in_specs=specs + [VMEM_SPEC] * (len(operands) - scalars),
        out_specs=tuple(VMEM_SPEC for _ in shapes),
        compiler_params=pltpu.CompilerParams(vmem_limit_bytes=40 * 1024 * 1024),
    )(*operands)


def carried(totals, reverse):
    count = lax.axis_size("dp")
    channels = totals.shape[-1]
    totals = totals.reshape(2, count, MICRO, channels)
    everything = jnp.stack([totals] + other_planes(totals))
    where = jnp.stack([lax.axis_index("dp"), lax.axis_index("section")]).astype(jnp.int32)

    def kernel(where_ref, totals_ref, carry_ref):
        carry_kernel(reverse, where_ref, totals_ref, carry_ref)

    (carry,) = in_vmem(kernel, [(count, MICRO, channels)], where, everything, scalars=1)
    return carry.reshape(count * MICRO, channels)


def gelu_product(states, side):
    return states * jax.nn.gelu(side)


def gated_gelu(gate_val, up_val):
    return jax.nn.gelu(gate_val) * up_val


def local(
    inputs,
    cotangent,
    resets,
    branch_in,
    gate_in,
    rec_out,
    rate_gate,
    input_gate,
    conv_taps,
    conv_bias,
    rate_bias,
    input_bias,
    decay_param,
    norm_rec,
    norm_mlp,
    mlp_gate,
    mlp_up,
    mlp_down,
):
    planes = lax.axis_size("section")
    count = lax.axis_size("dp")
    rank = lax.axis_index("section")
    me = lax.axis_index("dp")
    block_rows = inputs.shape[1]
    length = block_rows // planes
    seq = resets.shape[1]
    rows = MICRO * length
    segments = MICRO * count
    tokens = segments * length
    own = R // count
    wide = F // count
    strip = D // count
    thin = strip // planes
    filler = D // 2 - BW // 2 - WIN - own
    order = jnp.array(meeting_order(count), jnp.int32)
    devices = jnp.bitwise_xor(me, order)

    small = jnp.concatenate(
        [
            norm_rec,
            norm_mlp,
            conv_taps.reshape(LAYERS, CONV * own),
            conv_bias,
        ],
        axis=1,
    )
    small_all = lax.all_gather(small, "dp", axis=0, tiled=False)
    own_begin = own * me
    first_block = jnp.minimum(own_begin // BW, H - 2)
    shift = own_begin - BW * first_block

    def small_whole(layer, begin, each):
        return small_all[:, layer, begin : begin + each].reshape(count * each)

    def packed_in(layer, shared):
        def cut(value, axis):
            if not shared:
                return value
            size = value.shape[axis] // planes
            return lax.dynamic_slice_in_dim(value, size * later_rank, size, axis)

        gates = cut(jnp.stack([rate_gate[layer], input_gate[layer]]), 2)
        blocks = []
        for device in range(count):
            begin, end, left, right = window_of(device, count)
            height = thin if shared else strip
            blocks.append(gates[:, left // BW : right // BW].reshape(height, -1))
        branch, gate, at = branch_in, gate_in, layer
        if shared:
            branch, gate, at = cut(branch_in[layer:], 1), cut(gate_in[layer:], 1), 0
        return packed_columns(branch, gate, jnp.stack(blocks), at, filler)

    def by_features(value):
        moved = value.reshape(MICRO, length, D)
        return lax.all_to_all(moved, "section", split_axis=2, concat_axis=1, tiled=True)

    both_ends = lax.all_to_all(
        jnp.concatenate([inputs, cotangent], axis=0), "section", 1, 2, tiled=True
    )
    stream, grad = both_ends[:MICRO].reshape(rows, D), both_ends[MICRO:].reshape(rows, D)
    top_grad_all = all_rows(grad)
    in_moved = [None] * LAYERS
    mlp_moved = [None] * LAYERS
    first_pack = packed_in(0, False)
    later_rank = after(rank, first_pack)[0]
    in_moved[0] = spread(after(first_pack, small_all, stream)[0])
    normed = low(rms_scale(high(stream), high(small_whole(0, 0, strip))))
    first_normed = gather_rows(normed)
    in_width = WIN + own + filler
    first_both = dot(first_normed, in_moved[0].reshape(D, -1)[:, :in_width])
    in_share = spread(after(packed_in(1, True), first_both)[0])
    in_moved[1] = lax.all_gather(in_share, "section", axis=1, tiled=True)
    mlp_moved[0] = spread(after(columns_apart(mlp_gate, mlp_up, 0, count), in_share)[0])
    def layer_weights(layer):
        in_weight = in_moved[layer].reshape(D, -1)
        blocks = in_weight[:, WIN + own + filler :]
        parts = planes if layer else 1
        blocks = blocks.reshape(count, parts, 2, 2, BW // count // parts, BW)
        blocks = blocks.transpose(2, 3, 0, 1, 4, 5).reshape(2, 2, BW, BW)
        in_weight = in_weight[:, : WIN + own + filler]
        empty = jnp.zeros((BW, BW), jnp.bfloat16)
        gate_weights = []
        for which in range(2):
            whole = jnp.concatenate(
                [
                    jnp.concatenate([blocks[which, 0], empty], axis=1),
                    jnp.concatenate([empty, blocks[which, 1]], axis=1),
                ],
                axis=0,
            )
            gate_weights.append(turned(turned(whole, 0, shift), 1, shift)[:, :own])
        taps = jnp.concatenate(
            [
                small_all[:, layer, 2 * strip :].reshape(count, CONV + 1, own),
            ],
            axis=0,
        )
        taps = taps.transpose(1, 0, 2).reshape(CONV + 1, R)
        taps = lax.dynamic_slice_in_dim(taps, BW * first_block, WIN, 1)
        taps = high(turned(taps, 1, shift))
        return (
            {
                "in": in_weight,
                "gates": jnp.concatenate(gate_weights, axis=1),
                "out": rec_out[layer],
                "taps": taps[:CONV],
                "bias": taps[CONV],
                "rate_bias": high(rate_bias[layer]),
                "input_bias": high(input_bias[layer]),
                "decay": high(decay_param[layer]),
                "norm_rec": high(small_whole(layer, 0, strip)),
                "norm_mlp": high(small_whole(layer, strip, strip)),
                "down": mlp_down[layer],
            }
        )

    keep = (1 - resets).astype(jnp.float32)
    padded = jnp.concatenate(
        [
            jnp.ones((MICRO, MARGIN), jnp.float32),
            keep,
            jnp.zeros((MICRO, length), jnp.float32),
        ],
        axis=1,
    )
    reach = 2 * MARGIN
    window = jnp.concatenate(
        [
            padded[:, :seq].reshape(MICRO, count, planes, length),
            padded[:, length : length + seq].reshape(MICRO, count, planes, length)[..., :reach],
        ],
        axis=3,
    )
    window = lax.dynamic_index_in_dim(window, rank, 2, keepdims=False)
    same = (devices[:, None] == jnp.arange(count)[None, :]).astype(jnp.float32)
    window = jnp.einsum("pj,mjr->pmr", same, window, precision=lax.Precision.HIGHEST)
    window = window.reshape(segments, length + reach)
    usable = [jnp.ones((segments, length + MARGIN, 1), jnp.float32)]
    for lag in range(1, CONV):
        begin = MARGIN - lag + 1
        usable.append(usable[-1] * window[:, begin : begin + length + MARGIN, None])
    carry_mask = window[:, MARGIN : MARGIN + length, None]

    edge_from = {}
    for step, plane in ((1, 0), (-1, planes - 1)):
        wanted = devices - jnp.where(rank == plane, step, 0)
        edge_from[step] = (wanted[:, None] == devices[None, :]).astype(jnp.float32)

    def edge(rows_out, step):
        came = lax.ppermute(
            rows_out, "section", [(at, (at + step) % planes) for at in range(planes)]
        )
        flat = came.reshape(count, -1)
        chosen = edge_from[step]
        moved = sum(chosen[:, q : q + 1] * flat[q][None] for q in range(count))
        return moved.reshape(rows_out.shape)

    def lru_parts(weight):
        rate = RATE_SCALE * jax.nn.softplus(-weight["decay"])
        return rate

    def rec_forward(section_in, weight, normed, both, late):
        if normed is None:
            normed = gather_rows(low(rms_scale(high(section_in), weight["norm_rec"])))
            both = dot(normed, weight["in"])
        branch = both[:, :WIN].reshape(segments, length, WIN)
        side = both[:, WIN : WIN + own].reshape(segments, length, own)
        extended = jnp.concatenate([edge(branch[:, length - MARGIN :], 1), branch], axis=1)
        conved = weight["bias"] + weight["taps"][0] * branch
        for lag in range(1, CONV):
            conved = (
                conved
                + weight["taps"][lag]
                * usable[lag][:, :length]
                * extended[:, MARGIN - lag : MARGIN - lag + length]
            )
        conv_low = low(conved).reshape(tokens, WIN)
        raw = dot(conv_low, weight["gates"])
        rate_sig = jax.nn.sigmoid(raw[:, :own] + weight["rate_bias"])
        input_sig = jax.nn.sigmoid(raw[:, own:] + weight["input_bias"])
        rate_sig = rate_sig.reshape(segments, length, own)
        input_sig = input_sig.reshape(segments, length, own)
        conved = conved[:, :, :own]
        decays = jnp.exp(-lru_parts(weight) * rate_sig) * carry_mask
        root = jnp.sqrt(1.0 + LRU_EPS - decays * decays)
        drives = root * input_sig * conved
        shape = (segments, length, own)
        cumulative, partial = in_vmem(forward_scan_kernel, [shape, shape], decays, drives)
        carry = carried(jnp.stack([cumulative[:, -1], partial[:, -1]]), False)
        states = partial + cumulative * carry[:, None]
        mixture = low(gelu_product(states, side)).reshape(tokens, own)
        mixture = after(mixture, *late)[0]
        result = high(section_in) + scatter_product(
            lambda left: dot(left, weight["out"]), mixture
        )
        kept = {
            "section_in": section_in,
            "normed": normed,
            "extended": extended,
            "side": side,
            "conved": conved,
            "conv_low": conv_low,
            "rate_sig": rate_sig,
            "input_sig": input_sig,
            "decays": decays,
            "root": root,
            "carry": carry,
            "states": states,
            "mixture": mixture,
        }
        return low(result), kept

    def mlp_forward(section_in, weight, late):
        normed = low(rms_scale(high(section_in), weight["norm_mlp"]))
        here = normed
        normed = gather_rows(normed)
        both = dot(normed, weight["mlp"])
        gate_val, up_val = both[:, :wide], both[:, wide:]
        hidden = after(low(gated_gelu(gate_val, up_val)), *late)[0]
        result = high(section_in) + scatter_product(
            lambda left: dot(left, weight["down"]), hidden
        )
        kept = {
            "section_in": section_in,
            "normed": here,
            "hidden": hidden,
            "gate_val": gate_val,
            "up_val": up_val,
        }
        return low(result), kept

    def mlp_backward(grad, weight, kept):
        grad_all = gather_rows(grad)
        grad_hidden = dot_nt(grad_all, weight["down"])
        _, pull = jax.vjp(gated_gelu, kept["gate_val"], kept["up_val"])
        gate_grad, up_grad = pull(grad_hidden)
        both = jnp.concatenate([low(gate_grad), low(up_grad)], axis=1)
        grad_normed = scatter_product(lambda left: dot_nt(left, weight["mlp"]), both)
        _, pull = jax.vjp(rms_scale, high(kept["section_in"]), weight["norm_mlp"])
        grad_in, norm_grad = pull(grad_normed)
        return low(grad_in + high(grad)), {"norm_mlp": norm_grad}

    def rec_backward(grad, weight, kept, early):
        grad_all = gather_rows(grad)
        shape = (segments, length, own)
        grad_mixture = dot_nt(grad_all, weight["out"]).reshape(shape)
        _, pull = jax.vjp(gelu_product, kept["states"], kept["side"])
        grad_states0, grad_side = pull(grad_mixture)
        decays, root = kept["decays"], kept["root"]
        reached, partial, top = in_vmem(
            backward_scan_kernel,
            [shape, shape, (2, segments, own)],
            decays,
            grad_states0,
        )
        carry = carried(after(top, *early)[0], True)
        grad_states = partial + reached * carry[:, None]
        previous = jnp.concatenate([kept["carry"][:, None], kept["states"][:, :-1]], axis=1)
        conved, rate_sig, input_sig = kept["conved"], kept["rate_sig"], kept["input_sig"]
        grad_decays = grad_states * (previous - input_sig * conved * decays / root)
        slope = grad_decays * decays * rate_sig
        rate_grad = slope * (-lru_parts(weight)) * (1.0 - rate_sig)
        input_grad = grad_states * root * conved * input_sig * (1.0 - input_sig)
        raw_grad = low(
            jnp.concatenate([rate_grad, input_grad], axis=2).reshape(tokens, 2 * own)
        )
        spare = jnp.zeros((segments, length, WIN - own), jnp.float32)
        conv_grad = jnp.concatenate([grad_states * root * input_sig, spare], axis=2)
        conv_grad = conv_grad + dot_nt(raw_grad, weight["gates"]).reshape(segments, length, WIN)
        longer = jnp.concatenate([conv_grad, edge(conv_grad[:, :MARGIN], -1)], axis=1)
        branch_grad = weight["taps"][0] * conv_grad
        taps_grad = [jnp.sum(kept["extended"][:, MARGIN:] * conv_grad, axis=(0, 1))]
        for lag in range(1, CONV):
            branch_grad = (
                branch_grad
                + weight["taps"][lag]
                * usable[lag][:, lag : lag + length]
                * longer[:, lag : lag + length]
            )
            taps_grad.append(
                jnp.sum(
                    usable[lag][:, :length]
                    * kept["extended"][:, MARGIN - lag : MARGIN - lag + length]
                    * conv_grad,
                    axis=(0, 1),
                )
            )
        both = low(
            jnp.concatenate(
                [branch_grad, grad_side, jnp.zeros((segments, length, filler), jnp.float32)],
                axis=2,
            ).reshape(tokens, WIN + own + filler)
        )
        grad_normed = scatter_product(lambda left: dot_nt(left, weight["in"]), both)
        _, pull = jax.vjp(rms_scale, high(kept["section_in"]), weight["norm_rec"])
        grad_in, norm_grad = pull(grad_normed)
        terms = {
            "in": dot_tn(kept["normed"], both),
            "out": dot_tn(kept["mixture"], grad_all),
            "gates": dot_tn(kept["conv_low"], raw_grad),
            "taps": jnp.stack(taps_grad + [jnp.sum(conv_grad, axis=(0, 1))]),
            "rate_bias": jnp.sum(rate_grad, axis=(0, 1)),
            "input_bias": jnp.sum(input_grad, axis=(0, 1)),
            "decay": jnp.sum(slope, axis=(0, 1)) * RATE_SCALE * jax.nn.sigmoid(-weight["decay"]),
            "norm_rec": norm_grad,
            "in_grads": both,
        }
        return low(grad_in + high(grad)), terms

    def mlp_gradients(normed, grad_all, weight):
        both = dot(normed, weight["mlp"])
        product, pull = jax.vjp(gated_gelu, both[:, :wide], both[:, wide:])
        gate_grad, up_grad = pull(dot_nt(grad_all, weight["down"]))
        both_grad = jnp.concatenate([low(gate_grad), low(up_grad)], axis=1)
        return low(dot_tn(normed, both_grad)), dot_tn(low(product), grad_all)

    def to_rows(part):
        return spread(part.reshape(count, strip, 2 * wide))

    def rec_shares(terms):
        each = BW // count // planes
        blocks = []
        for which in range(2):
            square = jnp.concatenate(
                [
                    terms["gates"][:, which * own : (which + 1) * own],
                    jnp.zeros((WIN, WIN - own), jnp.float32),
                ],
                axis=1,
            )
            square = turned(turned(square, 0, -shift), 1, -shift)
            blocks.append(jnp.stack([square[:BW, :BW], square[BW:, BW:]]))
        blocks = low(jnp.stack(blocks)).reshape(2, 2, count, planes, each, 2, BW // 2)
        blocks = blocks.transpose(3, 2, 0, 1, 4, 5, 6).reshape(planes, count, 8 * each, BW // 2)
        blocks = blocks.reshape(planes, count, thin, -1)
        mixed = low(terms["in"]).reshape(count, planes, thin, WIN + own + filler)
        mixed = jnp.concatenate([mixed.transpose(1, 0, 2, 3), blocks], axis=3)
        width = mixed.shape[-1]
        out = low(terms["out"]).reshape(planes, own // planes, D)
        flat = jnp.concatenate(
            [mixed.reshape(planes, count * thin, width), lane_blocks(out, width)], axis=1
        )
        return flat

    def rec_pieces(flat):
        each = BW // count // planes
        width = WIN + own + filler + 8 * each * (BW // 2) // thin
        out = whole_rows(flat[count * thin :], own // planes)
        mine = spread(flat[: count * thin].reshape(count, thin, width))
        blocks = mine[:, :, WIN + own + filler :].reshape(count, 2, 2, each, BW)
        mine = high(mine)
        gate = low(mine[:, :, WIN : WIN + own]).transpose(1, 0, 2).reshape(thin, R)
        branch = mine[:, :, :own].transpose(1, 0, 2).reshape(thin, R)
        for device in range(count):
            begin, end, left, right = window_of(device, count)
            if right > end:
                piece = mine[device, :, own : own + right - end]
                branch = branch + jnp.pad(piece, ((0, 0), (end, R - right)))
            if begin > left:
                piece = mine[device, :, own + right - end : WIN]
                branch = branch + jnp.pad(piece, ((0, 0), (left, R - begin)))
        totals = [0.0] * H
        for device in range(count):
            first = window_of(device, count)[2] // BW
            for at in range(2):
                totals[first + at] = totals[first + at] + high(blocks[device, :, at])
        gates = low(jnp.stack(totals, axis=1))
        return jnp.concatenate(
            [
                lane_blocks(low(branch), WIN),
                lane_blocks(gate, WIN),
                lane_blocks(out, WIN),
                lane_blocks(gates.reshape(-1, 2 * BW), WIN),
            ],
            axis=0,
        )

    def rec_gradients(flat):
        each = BW // count // planes
        sizes = [thin * R // WIN, thin * R // WIN, own // planes * D // WIN]
        at = [0, sizes[0], sizes[0] + sizes[1], sum(sizes)]
        branch = whole_rows(flat[:, at[0] : at[1]], thin).reshape(strip, R)
        gate = whole_rows(flat[:, at[1] : at[2]], thin).reshape(strip, R)
        out = whole_rows(flat[:, at[2] : at[3]], own // planes).reshape(own, D)
        gates = flat[:, at[3] :].reshape(planes, 2, H, each, BW)
        gates = gates.transpose(1, 2, 0, 3, 4).reshape(2, H, BW // count, BW)
        return branch, gate, out, gates[0], gates[1]

    def small_gradients(terms):
        taps = turned(terms["taps"], 1, -shift)
        taps = lax.dynamic_update_slice(
            jnp.zeros((CONV + 1, R), jnp.float32), taps, (0, BW * first_block)
        )
        owned = jnp.stack([terms["rate_bias"], terms["input_bias"], terms["decay"]])
        owned = lax.dynamic_update_slice(
            jnp.zeros((3, R), jnp.float32), owned, (0, own_begin)
        )
        channels = jnp.concatenate([taps, owned], axis=0)
        norms = jnp.stack([terms["norm_rec"], terms["norm_mlp"]])
        pack = jnp.concatenate(
            [
                channels.reshape(CONV + 4, count, own).transpose(1, 0, 2).reshape(count, -1),
                norms.reshape(2, count, strip).transpose(1, 0, 2).reshape(count, -1),
            ],
            axis=1,
        )
        mine = jnp.sum(spread(pack), axis=0)
        mine = mine.reshape(-1, 128)
        mine = (mine + sum(other_planes(mine))).reshape(-1)
        channels = mine[: (CONV + 4) * own].reshape(CONV + 4, own)
        norms = mine[(CONV + 4) * own :].reshape(2, strip)
        return channels, norms

    weights = [layer_weights(0)]
    weights[0]["mlp"] = mlp_moved[0].reshape(D, 2 * wide)
    kept = []
    everyone = [None] * LAYERS
    top = LAYERS - 1
    for layer in range(LAYERS):
        weight = weights[layer]
        first = layer == 0
        stream, kept_rec = rec_forward(
            stream,
            weight,
            first_normed if first else None,
            first_both if first else None,
            [top_grad_all] if first else [],
        )
        if first:
            shares = [
                lax.dynamic_slice_in_dim(part[1:], thin * rank, thin, 1)
                for part in (mlp_gate, mlp_up)
            ]
            share = spread(after(columns_apart(*shares, 0, count), mlp_moved[0])[0])
            share = after(share, in_moved[1])[0]
            mlp_moved[1] = lax.all_gather(share, "section", axis=1, tiled=True)
            weights.append(layer_weights(1))
        else:
            everyone[0] = all_rows(after(kept[0][1]["normed"], kept_rec["mixture"])[0])
        stream, kept_mlp = mlp_forward(stream, weight, [share] if first else [])
        if first:
            weights[1]["mlp"] = mlp_moved[1].reshape(D, 2 * wide)
        else:
            everyone[1] = all_rows(after(kept_mlp["normed"], stream)[0])
        kept.append((kept_rec, kept_mlp))
    output = by_features(stream)
    mlp_downs = [None] * LAYERS
    mlp_rows = [None] * LAYERS
    rec_flat = [None] * LAYERS
    smalls = [None] * LAYERS

    grad_in = grad
    grad, mlp_terms = mlp_backward(grad_in, weights[1], kept[1][1])
    ins1, mlp_downs[1] = mlp_gradients(everyone[1], top_grad_all, weights[1])
    grad, everyone[0] = after(grad, everyone[0])
    grad, terms = rec_backward(grad, weights[1], kept[1][0], [output])
    grad, everyone[1] = after(grad, everyone[1])
    flat = section_sum(rec_shares(terms))
    smalls[1] = small_gradients({**mlp_terms, **terms})
    mlp_rows[1] = to_rows(ins1)

    grad_in = grad
    grad_mid, mlp_terms = mlp_backward(grad_in, weights[0], kept[0][1])
    pieces1 = rec_pieces(after(flat, grad_mid)[0])
    grad_all = all_rows(grad_in)
    grad, terms = rec_backward(grad_mid, weights[0], kept[0][0], [pieces1])
    input_grad = by_features(grad)
    flat = rec_shares(terms)
    grad_all = after(grad_all, flat)[0]
    flat = section_sum(flat)
    rec_flat[1] = lax.all_gather(after(pieces1, flat)[0], "section", axis=0, tiled=False)
    smalls[0] = small_gradients({**mlp_terms, **terms})
    ins0, mlp_downs[0] = mlp_gradients(everyone[0], grad_all, weights[0])
    joined = [joined_rows(mlp_rows[1], which, 1, LAYERS, None) for which in range(2)]
    flat = after(flat, ins0, mlp_rows[1], input_grad)[0]
    pieces0 = rec_pieces(flat)
    rec_flat[0] = lax.all_gather(pieces0, "section", axis=0, tiled=False)
    mlp_rows[0] = to_rows(after(ins0, pieces0)[0])
    mlp_results = tuple(
        joined_rows(mlp_rows[0], which, 0, LAYERS, joined[which]) for which in range(2)
    ) + (jnp.stack(mlp_downs),)
    rec_flat[0] = after(rec_flat[0], *mlp_results, input_grad, *smalls[0])[0]
    results = []
    for layer in range(LAYERS):
        channels, norms = smalls[layer]
        results.append(
            rec_gradients(rec_flat[layer])
            + (
                channels[:CONV],
                channels[CONV],
                channels[CONV + 1],
                channels[CONV + 2],
                channels[CONV + 3],
                norms[0],
                norms[1],
            )
        )
    stacked = tuple(high(jnp.stack(parts)) for parts in zip(*results))
    return (output, input_grad) + stacked + mlp_results


def solution(mesh):
    return jax.shard_map(
        local,
        mesh=mesh,
        in_specs=(
            P(None, "dp", "section"),
            P(None, "dp", "section"),
            P(),
            P(None, "dp", None),
            P(None, "dp", None),
            P(None, "dp", None),
            P(None, None, "dp", None),
            P(None, None, "dp", None),
            P(None, None, "dp"),
            P(None, "dp"),
            P(None, "dp"),
            P(None, "dp"),
            P(None, "dp"),
            P(None, "dp"),
            P(None, "dp"),
            P(None, "dp", None),
            P(None, "dp", None),
            P(None, "dp", None),
        ),
        out_specs=(
            P(None, "dp", "section"),
            P(None, "dp", "section"),
            P(None, "dp", None),
            P(None, "dp", None),
            P(None, "dp", None),
            P(None, None, "dp", None),
            P(None, None, "dp", None),
            P(None, None, "dp"),
            P(None, "dp"),
            P(None, "dp"),
            P(None, "dp"),
            P(None, "dp"),
            P(None, "dp"),
            P(None, "dp"),
            P(None, "dp", None),
            P(None, "dp", None),
            P(None, "dp", None),
        ),
        check_vma=False,
    )
```
